256 devices in a mesh: row: 16 (over z_lo, y, core), col: 16 (over z_hi, x).
Axes of the slice: x: 4, y: 4, z: 8 (z_hi: 4, z_lo: 2; z = z_hi * 2 + z_lo), core: 2. Of those that a mesh axis runs over, the one named last changes fastest.
Arguments:
- source_desc: bfloat16 [32768, 64], P('row', 'col'), may hold values from -9 to 9
- target_desc: bfloat16 [32768, 64], P('col'), may hold values from -9 to 9
- source_mass: bfloat16 [32768], P('row'), may hold values from 0.099609375 to 10
- target_mass: bfloat16 [32768], P('col'), may hold values from 0.099609375 to 10
Outputs:
- cross_source: float32 [32768], P('row')
- cross_target: float32 [32768], P('col')
- self_source: float32 [32768], P('row')
- self_target: float32 [32768], P('col')
The draws below stay inside these ranges and needn't reach their ends.
All inputs are finite; a program needn't handle non-finite values.
Results may differ from the reference program's by a relative error of at most 0.0003.
Values may be sent and summed in bfloat16 or wider, within the bound.
A program may use at most 64 MiB of HBM per device.

```python
import math
import jax
import jax.numpy as jnp
from jax import lax

C = 64
ITERS = 2
NX = 32768
NY = 32768


def descriptor_values(key, row_count, residue, offset):
    first_key = jax.random.fold_in(key, 0)
    values = jnp.clip(jax.random.normal(first_key, (row_count, C), jnp.float32), -6.0, 6.0) * (2.0 * C) ** (-0.5)
    position = jnp.arange(row_count, dtype=jnp.float32) / row_count
    factor = jnp.exp(position * math.log(3.0))[:, None]
    values = values * factor
    marked = (jnp.arange(row_count) % 64 == residue).astype(jnp.float32)[:, None]
    values = values + marked * offset
    return values.astype(jnp.bfloat16)


def draw_source_desc(key, part):
    return descriptor_values(key, NX, 5, 1.5)


def draw_target_desc(key, part):
    return descriptor_values(jax.random.fold_in(key, 7), NY, 37, -1.5)


def level_of(own_key, shape, cuts, smallest, top_value):
    factor_of, own = 1.0, jax.random.fold_in(own_key, 6)
    for dim, shards_of in cuts:
        draws = jnp.exp(jax.random.uniform(jax.random.fold_in(own, dim), (shards_of,), jnp.float32, smallest / len(cuts), top_value / len(cuts)))
        factor_of = factor_of * jnp.repeat(draws, shape[dim] // shards_of).reshape([-1 if axis == dim else 1 for axis in range(len(shape))])
    return factor_of


def setup_inputs(seed: int = 0) -> dict:
    key_list = jax.random.split(jax.random.key(seed), 5)
    return {
        "source_desc": draw_source_desc(jax.random.fold_in(key_list[4], 71), 0),
        "target_desc": draw_target_desc(jax.random.fold_in(key_list[4], 71), 0),
        "source_mass": jnp.clip(jnp.exp(math.log(10.0) - 4.609084 * jax.random.uniform(key_list[2], (NX,), jnp.float32) ** level_of(key_list[2], (NX,), ((0, 16),), -0.2, 0.2)), 0.099609375, 10.0).astype(jnp.bfloat16),
        "target_mass": jnp.clip(jnp.exp(math.log(10.0) - 4.609084 * jax.random.uniform(key_list[3], (NY,), jnp.float32) ** level_of(key_list[3], (NY,), ((0, 16),), -0.2, 0.2)), 0.099609375, 10.0).astype(jnp.bfloat16),
    }


EPSILON = 0.25
REACH = 1.0
DAMPING = 1.0 / (1.0 + EPSILON / REACH)


def half_norms(points):
    wide = points.astype(jnp.float32)
    return 0.5 * jnp.sum(wide * wide, axis=1)


def tile_stats(left_desc, right_desc, left_norm, right_norm, left_weight, right_weight, want_rows, want_cols):
    count = left_desc.shape[0]
    block = math.gcd(512, count)
    blocks = count // block
    width = left_desc.shape[1]
    right_count = right_desc.shape[0]
    inputs = (left_desc.reshape(blocks, block, width), left_norm.reshape(blocks, block), left_weight.reshape(blocks, block))

    def advance(carry, pieces):
        piece_desc, piece_norm, piece_weight = pieces
        product = lax.dot_general(piece_desc, right_desc, (((1,), (1,)), ((), ())), preferred_element_type=jnp.float32)
        scaled = (piece_norm[:, None] + right_norm[None, :] - product) / EPSILON
        emitted = ()
        if want_rows:
            row_score = right_weight[None, :] - scaled
            row_top = jnp.max(row_score, axis=1)
            row_total = jnp.sum(jnp.exp(row_score - row_top[:, None]), axis=1)
            emitted = (row_top, row_total)
        if want_cols:
            col_top, col_total = carry
            col_score = piece_weight[:, None] - scaled
            fresh_top = jnp.maximum(col_top, jnp.max(col_score, axis=0))
            col_total = col_total * jnp.exp(col_top - fresh_top) + jnp.sum(jnp.exp(col_score - fresh_top[None, :]), axis=0)
            carry = (fresh_top, col_total)
        return carry, emitted

    if want_cols:
        start = (jnp.full((right_count,), -jnp.inf, jnp.float32), jnp.zeros((right_count,), jnp.float32))
    else:
        start = ()
    carry, emitted = lax.scan(advance, start, inputs)
    rows_out = (emitted[0].reshape(count), emitted[1].reshape(count)) if want_rows else None
    cols_out = carry if want_cols else None
    return rows_out, cols_out


def reference(source_desc, target_desc, source_mass, target_mass):
    source_log = jnp.log(source_mass.astype(jnp.float32))
    target_log = jnp.log(target_mass.astype(jnp.float32))
    source_norm = half_norms(source_desc)
    target_norm = half_norms(target_desc)
    cross_source = jnp.zeros(source_log.shape, jnp.float32)
    cross_target = jnp.zeros(target_log.shape, jnp.float32)
    self_source = jnp.zeros(source_log.shape, jnp.float32)
    self_target = jnp.zeros(target_log.shape, jnp.float32)
    for iteration in range(ITERS):
        cross_rows, cross_cols = tile_stats(source_desc, target_desc, source_norm, target_norm, source_log + cross_source / EPSILON, target_log + cross_target / EPSILON, True, True)
        source_rows, unused_a = tile_stats(source_desc, source_desc, source_norm, source_norm, source_log + self_source / EPSILON, source_log + self_source / EPSILON, True, False)
        target_rows, unused_b = tile_stats(target_desc, target_desc, target_norm, target_norm, target_log + self_target / EPSILON, target_log + self_target / EPSILON, True, False)
        fresh_cs = -EPSILON * (cross_rows[0] + jnp.log(cross_rows[1]))
        fresh_ct = -EPSILON * (cross_cols[0] + jnp.log(cross_cols[1]))
        fresh_ss = -EPSILON * (source_rows[0] + jnp.log(source_rows[1]))
        fresh_st = -EPSILON * (target_rows[0] + jnp.log(target_rows[1]))
        cross_source = 0.5 * cross_source + 0.5 * DAMPING * fresh_cs
        cross_target = 0.5 * cross_target + 0.5 * DAMPING * fresh_ct
        self_source = 0.5 * self_source + 0.5 * DAMPING * fresh_ss
        self_target = 0.5 * self_target + 0.5 * DAMPING * fresh_st
    return (cross_source, cross_target, self_source, self_target)
```

```python
import functools
import math

import jax
import jax.numpy as jnp
from jax import lax
from jax.experimental import pallas as pl
from jax.experimental.pallas import tpu as pltpu
from jax.sharding import PartitionSpec as P

MESH = pl.DeviceIdType.MESH
EPSILON = 0.25
REACH = 1.0
DAMPING = 1.0 / (1.0 + EPSILON / REACH)
LOG2E = math.log2(math.e)
LN2 = math.log(2.0)
SCALE = LOG2E / EPSILON
STEP = -0.5 * DAMPING
OUT = -0.5 * DAMPING * EPSILON * LN2
LANES = 128
F32 = jnp.float32
BF16 = jnp.bfloat16


def split3(value):
    high = value.astype(BF16).astype(F32)
    rest = value - high
    middle = rest.astype(BF16).astype(F32)
    low = (rest - middle).astype(BF16).astype(F32)
    return high, middle, low


def lane_block(k):
    return pl.ds(pl.multiple_of(k * LANES, LANES), LANES)


def side_rows(first, second, count):
    index = lax.broadcasted_iota(jnp.int32, (count, LANES), 0)
    rows = jnp.zeros((count, LANES), F32)
    for position, piece in enumerate(tuple(first) + tuple(second)):
        rows = jnp.where(index == position, piece, rows)
    return rows


def half_norm(points):
    return 0.5 * jnp.sum(points * points, axis=0, keepdims=True)


def right_block(b_ref, k, points):
    channels = points.shape[0]
    block = lane_block(k)
    narrow = points.astype(BF16)
    for copy in range(3):
        b_ref[copy * channels : (copy + 1) * channels, block] = narrow
    one = jnp.ones((1, LANES), F32)
    rows = side_rows((one, one, one), split3(-SCALE * half_norm(points)), 256 - 3 * channels)
    b_ref[3 * channels : 256, block] = rows.astype(BF16)


def left_block(a_ref, k, points, weight, whole):
    channels = points.shape[0]
    rows = pl.ds(pl.multiple_of(k * LANES, LANES), LANES)
    high, middle, low = split3(SCALE * points)
    if whole:
        a_ref[rows, 0:LANES] = jnp.concatenate([high, middle], axis=0).T.astype(BF16)
    one = jnp.ones((1, LANES), F32)
    side = side_rows(split3(weight - SCALE * half_norm(points)), (one, one, one), LANES - channels)
    a_ref[rows, LANES : 2 * LANES] = jnp.concatenate([low, side], axis=0).T.astype(BF16)


WIDE = 256
CHUNK = 256


def fold(value, op):
    return op(value.reshape(value.shape[0] // 8, 8, value.shape[1]), axis=0)


def emit(out_ref, j, row):
    for t in range(WIDE // LANES):
        out_ref[j * (WIDE // LANES) + t] = row[:, t * LANES : (t + 1) * LANES]


def lse_pass(a_ref, b_ref, m0, m1, out_ref):
    count = a_ref.shape[0]
    blocks = b_ref.shape[1] // WIDE
    chunks = count // CHUNK

    def product(j, i, m_ref):
        columns = pl.ds(pl.multiple_of(j * WIDE, WIDE), WIDE)
        part = jnp.dot(
            a_ref[i * CHUNK : (i + 1) * CHUNK, :], b_ref[:, columns], preferred_element_type=F32
        )
        m_ref[i * CHUNK : (i + 1) * CHUNK, :] = part
        return fold(part, jnp.max)

    def both(j, top, m_ref, next_j, next_ref):
        top = jnp.max(top, axis=0, keepdims=True)
        total = jnp.zeros((8, WIDE), F32)
        fresh = jnp.full((8, WIDE), -jnp.inf, F32)
        for i in range(chunks):
            fresh = jnp.maximum(fresh, product(next_j, i, next_ref))
            part = m_ref[i * CHUNK : (i + 1) * CHUNK, :]
            total = total + fold(jnp.exp2(part - top), jnp.sum)
        emit(out_ref, j, top + jnp.log2(jnp.sum(total, axis=0, keepdims=True)))
        return fresh

    top = jnp.full((8, WIDE), -jnp.inf, F32)
    for i in range(chunks):
        top = jnp.maximum(top, product(0, i, m0))

    def step(t, top):
        j = 2 * t
        top = both(j, top, m0, j + 1, m1)
        return both(j + 1, top, m1, lax.rem(j + 2, blocks), m0)

    lax.fori_loop(0, blocks // 2, step, top)


def kernel_pass(a_ref, b_ref, k_ref, out_ref):
    chunks = a_ref.shape[0] // CHUNK

    def step(j, carry):
        columns = pl.ds(pl.multiple_of(j * WIDE, WIDE), WIDE)
        total = jnp.zeros((8, WIDE), F32)
        for i in range(chunks):
            rows = slice(i * CHUNK, (i + 1) * CHUNK)
            part = jnp.exp2(jnp.dot(a_ref[rows, :], b_ref[:, columns], preferred_element_type=F32))
            k_ref[rows, columns] = part
            total = total + fold(part, jnp.sum)
        emit(out_ref, j, jnp.sum(total, axis=0, keepdims=True))
        return carry

    lax.fori_loop(0, b_ref.shape[1] // WIDE, step, 0)


def weighted_pass(q_ref, k_ref, out_ref):
    count = k_ref.shape[0]
    span = 8 * 16

    def column(j, carry):
        columns = pl.ds(pl.multiple_of(j * WIDE, WIDE), WIDE)

        def rows_step(i, total):
            rows = pl.ds(pl.multiple_of(i * span, span), span)
            part = k_ref[rows, columns]
            scale = q_ref[rows, :]
            return total + fold(part * jnp.concatenate([scale] * (WIDE // LANES), axis=1), jnp.sum)

        total = lax.fori_loop(0, count // span, rows_step, jnp.zeros((8, WIDE), F32), unroll=4)
        emit(out_ref, j, jnp.sum(total, axis=0, keepdims=True))
        return carry

    lax.fori_loop(0, k_ref.shape[1] // WIDE, column, 0)


def body_kernel(
    size,
    xs_ref,
    yt_ref,
    ms_ref,
    mt_ref,
    cs_ref,
    ct_ref,
    ss_ref,
    st_ref,
    xg,
    tg,
    sg,
    x32,
    ax,
    ay,
    bx,
    by,
    bs,
    bt,
    m0,
    m1,
    ks,
    kt,
    qx,
    qy,
    lms,
    lmt,
    parts,
    gathered,
    logs,
    send_sems,
    recv_sems,
):
    row, col = lax.axis_index("row"), lax.axis_index("col")
    place = {"row": row, "col": col}

    def peer(axis, k):
        return lax.rem(place[axis] + k, size)

    barrier = pltpu.get_barrier_semaphore()

    def greet(k, carry):
        for axis in ("row", "col"):
            pl.semaphore_signal(
                barrier, inc=1, device_id={axis: peer(axis, k)}, device_id_type=MESH
            )
        return carry

    lax.fori_loop(1, size, greet, 0)

    def send_all(op, axis, source_of, target):
        me = place[axis]

        def one(k, carry):
            other = peer(axis, k)
            pltpu.make_async_remote_copy(
                src_ref=source_of(other),
                dst_ref=target.at[me],
                send_sem=send_sems.at[op],
                recv_sem=recv_sems.at[op],
                device_id={axis: other},
                device_id_type=MESH,
            ).start()
            return carry

        lax.fori_loop(1, size, one, 0)

    def wait_all(sems, op, target):
        others = target.at[pl.ds(0, size - 1)]
        pltpu.make_async_copy(others, others, sems.at[op]).wait()

    pl.semaphore_wait(barrier, 2 * (size - 1))

    GX, GT, GS = 0, 1, 2
    send_all(GX, "col", lambda other: xs_ref, xg)
    send_all(GT, "col", lambda other: yt_ref.at[:, lane_block(row)], tg)

    log_mass_x = jnp.log2(ms_ref[...].astype(F32))
    log_mass_y = jnp.log2(mt_ref[...].astype(F32))
    for k in range(size):
        lms[k] = log_mass_x[k : k + 1, :]
        lmt[k] = log_mass_y[k : k + 1, :]

    def prepare_y(k, carry):
        points = yt_ref[:, lane_block(k)].astype(F32)
        right_block(by, k, points)
        left_block(ay, k, points, lmt[k], True)
        return carry

    lax.fori_loop(0, size, prepare_y, 0)
    tg[col] = yt_ref[:, lane_block(row)]
    xg[col] = xs_ref[...]

    wait_all(recv_sems, GX, xg)
    group = xs_ref.shape[0]
    for c in range(size):
        x32[c * group : (c + 1) * group, :] = xg[c].astype(F32)

    def prepare_x(k, carry):
        points = x32[:, lane_block(k)]
        right_block(bx, k, points)
        left_block(ax, k, points, lms[k], True)
        return carry

    lax.fori_loop(0, size, prepare_x, 0)
    channels = x32.shape[0]
    send_all(GS, "row", lambda other: bx.at[0:channels, lane_block(col)], sg)
    sg[row] = bx[0:channels, lane_block(col)]

    CR, CC, ST, SS = 0, 1, 2, 3
    FIRST_AXIS = ("col", "row", "col", "row")
    SECOND_AXIS = ("col", "row", "row", "col")

    def reduce_op(it, which):
        return 3 + 8 * it + which

    def gather_op(it, which):
        return 3 + 8 * it + 4 + which

    def send_parts(it, which):
        axis = FIRST_AXIS[which]
        part, inbox = parts.at[it, which], gathered.at[it, which]
        send_all(reduce_op(it, which), axis, lambda other: part.at[other], inbox)
        me = place[axis]
        inbox[me] = part[me]

    def combine(it, which):
        inbox = gathered.at[it, which]
        wait_all(recv_sems, reduce_op(it, which), inbox)
        values = inbox[...]
        if which in (CR, CC):
            top = jnp.max(values, axis=0)
            total = top + jnp.log2(jnp.sum(jnp.exp2(values - top[None]), axis=0))
        else:
            total = jnp.log2(jnp.sum(values, axis=0))
        axis = SECOND_AXIS[which]
        box = logs.at[it, which]
        me = place[axis]
        box[me] = total
        send_all(gather_op(it, which), axis, lambda other: box.at[me], box)

    def await_logs(it, which):
        wait_all(recv_sems, gather_op(it, which), logs.at[it, which])

    def prepare_right(b_ref, inbox):
        def step(k, carry):
            right_block(b_ref, k, inbox[k].astype(F32))
            return carry

        lax.fori_loop(0, size, step, 0)

    lse_pass(ay, bx, m0, m1, parts.at[0, CR])
    send_parts(0, CR)
    lse_pass(ax, by, m0, m1, parts.at[0, CC])
    send_parts(0, CC)
    wait_all(recv_sems, GT, tg)
    prepare_right(bt, tg)
    combine(0, CR)
    kernel_pass(ay, bt, kt, parts.at[0, ST])
    send_parts(0, ST)
    combine(0, CC)
    wait_all(recv_sems, GS, sg)
    prepare_right(bs, sg)
    kernel_pass(ax, bs, ks, parts.at[0, SS])
    send_parts(0, SS)
    combine(0, ST)
    await_logs(0, CR)
    await_logs(0, CC)

    def reweight(a_ref, b_ref, mass, which):
        def step(k, carry):
            points = b_ref[0:channels, lane_block(k)].astype(F32)
            left_block(a_ref, k, points, mass[k] + STEP * logs[0, which, k], False)
            return carry

        lax.fori_loop(0, size, step, 0)

    reweight(ay, by, lmt, CC)
    reweight(ax, bx, lms, CR)

    def lane_weights(q_ref, which):
        def step(k, carry):
            weight = jnp.exp2(STEP * logs[0, which, k])
            rows = pl.ds(pl.multiple_of(k * LANES, LANES), LANES)
            q_ref[rows, :] = jnp.broadcast_to(weight, (LANES, LANES)).T
            return carry

        lax.fori_loop(0, size, step, 0)

    def finish(which, out_ref):
        await_logs(1, which)
        out_ref[...] = (0.5 * OUT) * logs[0, which] + OUT * logs[1, which]

    lse_pass(ay, bx, m0, m1, parts.at[1, CR])
    send_parts(1, CR)
    combine(0, SS)
    lse_pass(ax, by, m0, m1, parts.at[1, CC])
    send_parts(1, CC)
    await_logs(0, ST)
    lane_weights(qy, ST)
    weighted_pass(qy, kt, parts.at[1, ST])
    send_parts(1, ST)
    combine(1, CR)
    combine(1, CC)
    await_logs(0, SS)
    lane_weights(qx, SS)
    weighted_pass(qx, ks, parts.at[1, SS])
    send_parts(1, SS)
    combine(1, ST)
    finish(CR, cs_ref)
    finish(CC, ct_ref)
    combine(1, SS)
    finish(ST, st_ref)
    finish(SS, ss_ref)

    wait_all(send_sems, GX, xg)
    wait_all(send_sems, GT, tg)
    wait_all(send_sems, GS, sg)
    for it in range(2):
        for which in range(4):
            wait_all(send_sems, reduce_op(it, which), gathered.at[it, which])
            wait_all(send_sems, gather_op(it, which), logs.at[it, which])


def body(size, source_desc, target_desc, source_mass, target_mass):
    count, group = source_desc.shape
    channels = target_desc.shape[1]
    vector = (size, 1, LANES)
    outs = pl.pallas_call(
        functools.partial(body_kernel, size),
        out_shape=[jax.ShapeDtypeStruct(vector, F32)] * 4,
        in_specs=[pl.BlockSpec(memory_space=pltpu.VMEM)] * 4,
        out_specs=[pl.BlockSpec(memory_space=pltpu.VMEM)] * 4,
        scratch_shapes=[
            pltpu.VMEM((size, group, count), BF16),
            pltpu.VMEM((size, channels, LANES), BF16),
            pltpu.VMEM((size, channels, LANES), BF16),
            pltpu.VMEM((channels, count), F32),
            pltpu.VMEM((count, 256), BF16),
            pltpu.VMEM((count, 256), BF16),
            pltpu.VMEM((256, count), BF16),
            pltpu.VMEM((256, count), BF16),
            pltpu.VMEM((256, count), BF16),
            pltpu.VMEM((256, count), BF16),
            pltpu.VMEM((count, WIDE), F32),
            pltpu.VMEM((count, WIDE), F32),
            pltpu.VMEM((count, count), F32),
            pltpu.VMEM((count, count), F32),
            pltpu.VMEM((count, LANES), F32),
            pltpu.VMEM((count, LANES), F32),
            pltpu.VMEM(vector, F32),
            pltpu.VMEM(vector, F32),
            pltpu.VMEM((2, 4) + vector, F32),
            pltpu.VMEM((2, 4) + vector, F32),
            pltpu.VMEM((2, 4) + vector, F32),
            pltpu.SemaphoreType.DMA((19,)),
            pltpu.SemaphoreType.DMA((19,)),
        ],
        compiler_params=pltpu.CompilerParams(
            collective_id=0, has_side_effects=True, vmem_limit_bytes=56 * 1024 * 1024
        ),
    )(
        source_desc.T,
        target_desc.T,
        source_mass.reshape(size, LANES),
        target_mass.reshape(size, LANES),
    )
    return tuple(out.reshape(count) for out in outs)


def solution(mesh):
    return jax.shard_map(
        functools.partial(body, mesh.shape["row"]),
        mesh=mesh,
        in_specs=(P("row", "col"), P("col", None), P("row"), P("col")),
        out_specs=(P("row"), P("col"), P("row"), P("col")),
        check_vma=False,
    )
```

```python
import functools
import math

import jax
import jax.numpy as jnp
from jax import lax
from jax.experimental import pallas as pl
from jax.experimental.pallas import tpu as pltpu
from jax.sharding import PartitionSpec as P

MESH = pl.DeviceIdType.MESH
EPSILON = 0.25
REACH = 1.0
DAMPING = 1.0 / (1.0 + EPSILON / REACH)
LOG2E = math.log2(math.e)
LN2 = math.log(2.0)
SCALE = LOG2E / EPSILON
STEP = -0.5 * DAMPING
OUT = -0.5 * DAMPING * EPSILON * LN2
LANES = 128
F32 = jnp.float32
BF16 = jnp.bfloat16


def split3(value):
    high = value.astype(BF16).astype(F32)
    rest = value - high
    middle = rest.astype(BF16).astype(F32)
    low = (rest - middle).astype(BF16).astype(F32)
    return high, middle, low


def lane_block(k):
    return pl.ds(pl.multiple_of(k * LANES, LANES), LANES)


def side_rows(first, second, count):
    index = lax.broadcasted_iota(jnp.int32, (count, LANES), 0)
    rows = jnp.zeros((count, LANES), F32)
    for position, piece in enumerate(tuple(first) + tuple(second)):
        rows = jnp.where(index == position, piece, rows)
    return rows


def half_norm(points):
    return 0.5 * jnp.sum(points * points, axis=0, keepdims=True)


def right_block(b_ref, k, points):
    channels = points.shape[0]
    block = lane_block(k)
    narrow = points.astype(BF16)
    for copy in range(3):
        b_ref[copy * channels : (copy + 1) * channels, block] = narrow
    one = jnp.ones((1, LANES), F32)
    rows = side_rows((one, one, one), split3(-SCALE * half_norm(points)), 256 - 3 * channels)
    b_ref[3 * channels : 256, block] = rows.astype(BF16)


def left_block(a_ref, k, points, weight, whole):
    channels = points.shape[0]
    rows = pl.ds(pl.multiple_of(k * LANES, LANES), LANES)
    high, middle, low = split3(SCALE * points)
    if whole:
        a_ref[rows, 0:LANES] = jnp.concatenate([high, middle], axis=0).T.astype(BF16)
    one = jnp.ones((1, LANES), F32)
    side = side_rows(split3(weight - SCALE * half_norm(points)), (one, one, one), LANES - channels)
    a_ref[rows, LANES : 2 * LANES] = jnp.concatenate([low, side], axis=0).T.astype(BF16)


CHUNK = 256
LSE_WIDE = 1024
KERNEL_WIDE = 1024
SUM_WIDE = 512
SPAN = 64
SUM_UNROLL = 8
UNROLL = 8


def fold(value, op):
    return op(value.reshape(value.shape[0] // 8, 8, value.shape[1]), axis=0)


def emit(out_ref, j, row, wide):
    per = wide // LANES
    for t in range(per):
        piece = row[:, t * LANES : (t + 1) * LANES]
        if len(out_ref.shape) == 3:
            out_ref[j * per + t] = piece
        else:
            out_ref[pl.ds(j * per + t, 1), :] = piece


def lse_pass(a_ref, b_ref, out_ref):
    wide = min(LSE_WIDE, b_ref.shape[1])
    chunks = a_ref.shape[0] // CHUNK

    def column(j, carry):
        columns = pl.ds(pl.multiple_of(j * wide, wide), wide)
        right = b_ref[:, columns]
        top = jnp.full((8, wide), -1e30, F32)
        total = jnp.zeros((8, wide), F32)
        for i in range(chunks):
            left = a_ref[i * CHUNK : (i + 1) * CHUNK, :]
            part = jnp.dot(left, right, preferred_element_type=F32)
            part = part.reshape(CHUNK // 8, 8, wide)
            fresh = jnp.maximum(top, jnp.max(part, axis=0))
            total = total * jnp.exp2(top - fresh) + jnp.sum(jnp.exp2(part - fresh[None]), axis=0)
            top = fresh
        peak = jnp.max(top, axis=0, keepdims=True)
        total = jnp.sum(total * jnp.exp2(top - peak), axis=0, keepdims=True)
        emit(out_ref, j, peak + jnp.log2(total), wide)
        return carry

    lax.fori_loop(0, b_ref.shape[1] // wide, column, 0)


def kernel_pass(a_ref, b_ref, k_ref, out_ref):
    wide = min(KERNEL_WIDE, b_ref.shape[1])
    chunks = a_ref.shape[0] // CHUNK

    def step(j, carry):
        columns = pl.ds(pl.multiple_of(j * wide, wide), wide)
        right = b_ref[:, columns]
        total = jnp.zeros((8, wide), F32)
        for i in range(chunks):
            rows = slice(i * CHUNK, (i + 1) * CHUNK)
            part = jnp.exp2(jnp.dot(a_ref[rows, :], right, preferred_element_type=F32))
            k_ref[rows, columns] = part
            total = total + fold(part, jnp.sum)
        emit(out_ref, j, jnp.sum(total, axis=0, keepdims=True), wide)
        return carry

    lax.fori_loop(0, b_ref.shape[1] // wide, step, 0)


def weighted_pass(q_ref, k_ref, out_ref):
    wide = min(SUM_WIDE, k_ref.shape[1])

    def column(j, carry):
        columns = pl.ds(pl.multiple_of(j * wide, wide), wide)

        def rows_step(i, total):
            rows = pl.ds(pl.multiple_of(i * SPAN, SPAN), SPAN)
            scale = jnp.concatenate([q_ref[rows, :]] * (wide // LANES), axis=1)
            return total + fold(k_ref[rows, columns] * scale, jnp.sum)

        start = jnp.zeros((8, wide), F32)
        total = lax.fori_loop(0, k_ref.shape[0] // SPAN, rows_step, start, unroll=SUM_UNROLL)
        emit(out_ref, j, jnp.sum(total, axis=0, keepdims=True), wide)
        return carry

    lax.fori_loop(0, k_ref.shape[1] // wide, column, 0)


CR, CC, ST, SS = 0, 1, 2, 3
GX, GT, GS = 0, 1, 2
OPS = 3 + 12


def body_kernel(
    size,
    xs_hbm,
    yt_hbm,
    ms_hbm,
    mt_hbm,
    out_ref,
    xs_ref,
    yt_ref,
    ms_ref,
    mt_ref,
    xg,
    tg,
    sg,
    x32,
    ax,
    ay,
    bx,
    by,
    bs,
    bt,
    ks,
    kt,
    qx,
    qy,
    lms,
    lmt,
    cross_parts,
    cross_inbox,
    cross_logs,
    self_parts,
    self_inbox,
    self_logs,
    local_sems,
    send_sems,
    recv_sems,
):
    row, col = lax.axis_index("row"), lax.axis_index("col")
    place = {"row": row, "col": col}

    def peer(axis, k):
        return lax.rem(place[axis] + k, size)

    barrier = pltpu.get_barrier_semaphore()

    def greet(k, carry):
        for axis in ("col", "row"):
            pl.semaphore_signal(
                barrier, inc=1, device_id={axis: peer(axis, k)}, device_id_type=MESH
            )
        return carry

    lax.fori_loop(1, size, greet, 0)

    loads = [
        pltpu.make_async_copy(source, target, local_sems.at[index])
        for index, (source, target) in enumerate(
            ((yt_hbm, yt_ref), (mt_hbm, mt_ref), (ms_hbm, ms_ref), (xs_hbm, xs_ref))
        )
    ]
    for load in loads:
        load.start()

    def send_all(op, axis, source_of, target):
        me = place[axis]

        def one(k, carry):
            other = peer(axis, k)
            pltpu.make_async_remote_copy(
                src_ref=source_of(other),
                dst_ref=target.at[me],
                send_sem=send_sems.at[op],
                recv_sem=recv_sems.at[op],
                device_id={axis: other},
                device_id_type=MESH,
            ).start()
            return carry

        lax.fori_loop(1, size, one, 0)

    def wait_all(sems, op, target):
        others = target.at[pl.ds(0, size - 1)]
        pltpu.make_async_copy(others, others, sems.at[op]).wait()

    def blocks(step):
        def run(k, carry):
            step(k)
            return carry

        lax.fori_loop(0, size, run, 0, unroll=UNROLL)

    for load in loads:
        load.wait()
    log_mass_x = jnp.log2(ms_ref[...].astype(F32))
    log_mass_y = jnp.log2(mt_ref[...].astype(F32))
    for k in range(size):
        lms[k] = log_mass_x[k : k + 1, :]
        lmt[k] = log_mass_y[k : k + 1, :]

    def prepare_y(k):
        points = yt_ref[:, lane_block(k)].astype(F32)
        right_block(by, k, points)
        left_block(ay, k, points, lmt[k], True)

    blocks(prepare_y)
    tg[col] = yt_ref[:, lane_block(row)]
    xg[col] = xs_ref[...]

    pl.semaphore_wait(barrier, 2 * (size - 1))
    send_all(GX, "col", lambda other: xs_ref, xg)
    send_all(GT, "col", lambda other: yt_ref.at[:, lane_block(row)], tg)

    wait_all(recv_sems, GX, xg)
    group = xs_ref.shape[0]
    for c in range(size):
        x32[c * group : (c + 1) * group, :] = xg[c].astype(F32)

    def prepare_x(k):
        points = x32[:, lane_block(k)]
        right_block(bx, k, points)
        left_block(ax, k, points, lms[k], True)

    blocks(prepare_x)
    channels = x32.shape[0]
    send_all(GS, "row", lambda other: bx.at[0:channels, lane_block(col)], sg)
    sg[row] = bx[0:channels, lane_block(col)]

    CROSS_AXIS = ("col", "row")

    def cross_op(it, which):
        return 3 + 2 * it + which

    def send_cross(it, which):
        axis = CROSS_AXIS[which]
        part, inbox = cross_parts.at[it, which], cross_inbox.at[it, which]
        send_all(cross_op(it, which), axis, lambda other: part, inbox)
        inbox[place[axis]] = part[...]

    def combine_cross(it, which):
        inbox = cross_inbox.at[it, which]
        wait_all(recv_sems, cross_op(it, which), inbox)
        values = inbox[...]
        top = jnp.max(values, axis=0)
        total = jnp.sum(jnp.exp2(values - top[None]), axis=0)
        cross_logs[it, which] = top + jnp.log2(total)

    FIRST_AXIS = {ST: "col", SS: "row"}
    SECOND_AXIS = {ST: "row", SS: "col"}

    def reduce_op(it, which):
        return 7 + 4 * it + which - ST

    def gather_op(it, which):
        return 9 + 4 * it + which - ST

    def send_self(it, which):
        axis = FIRST_AXIS[which]
        part, inbox = self_parts.at[it, which - ST], self_inbox.at[it, which - ST]
        send_all(reduce_op(it, which), axis, lambda other: part.at[other], inbox)
        me = place[axis]
        inbox[me] = part[me]

    def combine_self(it, which):
        inbox = self_inbox.at[it, which - ST]
        wait_all(recv_sems, reduce_op(it, which), inbox)
        axis = SECOND_AXIS[which]
        box = self_logs.at[it, which - ST]
        me = place[axis]
        box[me] = jnp.log2(jnp.sum(inbox[...], axis=0))
        send_all(gather_op(it, which), axis, lambda other: box.at[me], box)

    def await_self(it, which):
        wait_all(recv_sems, gather_op(it, which), self_logs.at[it, which - ST])

    def prepare_right(b_ref, inbox):
        blocks(lambda k: right_block(b_ref, k, inbox[k].astype(F32)))

    def reweight(a_ref, b_ref, mass, which):
        def step(k):
            points = b_ref[0:channels, lane_block(k)].astype(F32)
            weight = mass[k] + STEP * cross_logs[0, which, pl.ds(k, 1), :]
            left_block(a_ref, k, points, weight, False)

        blocks(step)

    def lane_weights(q_ref, which):
        def step(k):
            weight = jnp.exp2(STEP * self_logs[0, which - ST, k])
            rows = pl.ds(pl.multiple_of(k * LANES, LANES), LANES)
            q_ref[rows, :] = jnp.broadcast_to(weight, (LANES, LANES)).T

        blocks(step)

    def finish_self(which):
        await_self(1, which)
        for k in range(size):
            out_ref[which, k : k + 1, :] = (0.5 * OUT) * self_logs[0, which - ST, k] + OUT * (
                self_logs[1, which - ST, k]
            )

    def finish_cross(which):
        out_ref[which] = (0.5 * OUT) * cross_logs[0, which] + OUT * cross_logs[1, which]

    lse_pass(ax, by, cross_parts.at[0, CC])
    send_cross(0, CC)
    wait_all(recv_sems, GT, tg)
    prepare_right(bt, tg)
    kernel_pass(ay, bt, kt, self_parts.at[0, 0])
    send_self(0, ST)
    wait_all(recv_sems, GS, sg)
    prepare_right(bs, sg)
    kernel_pass(ax, bs, ks, self_parts.at[0, 1])
    send_self(0, SS)
    lse_pass(ay, bx, cross_parts.at[0, CR])
    send_cross(0, CR)
    combine_self(0, ST)
    combine_cross(0, CC)
    combine_self(0, SS)
    reweight(ay, by, lmt, CC)
    lse_pass(ay, bx, cross_parts.at[1, CR])
    send_cross(1, CR)
    await_self(0, ST)
    lane_weights(qy, ST)
    weighted_pass(qy, kt, self_parts.at[1, 0])
    send_self(1, ST)
    await_self(0, SS)
    lane_weights(qx, SS)
    weighted_pass(qx, ks, self_parts.at[1, 1])
    send_self(1, SS)
    combine_cross(0, CR)
    reweight(ax, bx, lms, CR)
    lse_pass(ax, by, cross_parts.at[1, CC])
    send_cross(1, CC)
    combine_self(1, ST)
    combine_self(1, SS)
    combine_cross(1, CR)
    finish_cross(CR)
    combine_cross(1, CC)
    finish_cross(CC)
    finish_self(ST)
    finish_self(SS)

    wait_all(send_sems, GX, xg)
    wait_all(send_sems, GT, tg)
    wait_all(send_sems, GS, sg)
    for it in range(2):
        for which in (CR, CC):
            wait_all(send_sems, cross_op(it, which), cross_inbox.at[it, which])
        for which in (ST, SS):
            wait_all(send_sems, reduce_op(it, which), self_inbox.at[it, which - ST])
            wait_all(send_sems, gather_op(it, which), self_logs.at[it, which - ST])


def unpack_kernel(all_ref, cs_ref, ct_ref, ss_ref, st_ref):
    cs_ref[...] = all_ref[CR]
    ct_ref[...] = all_ref[CC]
    ss_ref[...] = all_ref[SS]
    st_ref[...] = all_ref[ST]


def body(size, source_desc, target_desc, source_mass, target_mass):
    count, group = source_desc.shape
    channels = target_desc.shape[1]
    vector = (size, 1, LANES)
    flat = (size, LANES)
    whole = pl.BlockSpec(memory_space=pltpu.VMEM)
    packed = pl.pallas_call(
        functools.partial(body_kernel, size),
        out_shape=jax.ShapeDtypeStruct((4,) + flat, F32),
        in_specs=[pl.BlockSpec(memory_space=pl.ANY)] * 4,
        out_specs=whole,
        scratch_shapes=[
            pltpu.VMEM((group, count), BF16),
            pltpu.VMEM((channels, count), BF16),
            pltpu.VMEM(flat, BF16),
            pltpu.VMEM(flat, BF16),
            pltpu.VMEM((size, group, count), BF16),
            pltpu.VMEM((size, channels, LANES), BF16),
            pltpu.VMEM((size, channels, LANES), BF16),
            pltpu.VMEM((channels, count), F32),
            pltpu.VMEM((count, 256), BF16),
            pltpu.VMEM((count, 256), BF16),
            pltpu.VMEM((256, count), BF16),
            pltpu.VMEM((256, count), BF16),
            pltpu.VMEM((256, count), BF16),
            pltpu.VMEM((256, count), BF16),
            pltpu.VMEM((count, count), F32),
            pltpu.VMEM((count, count), F32),
            pltpu.VMEM((count, LANES), F32),
            pltpu.VMEM((count, LANES), F32),
            pltpu.VMEM(vector, F32),
            pltpu.VMEM(vector, F32),
            pltpu.VMEM((2, 2) + flat, F32),
            pltpu.VMEM((2, 2, size) + flat, F32),
            pltpu.VMEM((2, 2) + flat, F32),
            pltpu.VMEM((2, 2) + vector, F32),
            pltpu.VMEM((2, 2) + vector, F32),
            pltpu.VMEM((2, 2) + vector, F32),
            pltpu.SemaphoreType.DMA((4,)),
            pltpu.SemaphoreType.DMA((OPS,)),
            pltpu.SemaphoreType.DMA((OPS,)),
        ],
        compiler_params=pltpu.CompilerParams(
            collective_id=0, has_side_effects=True, vmem_limit_bytes=56 * 1024 * 1024
        ),
    )(
        source_desc.T,
        target_desc.T,
        source_mass.reshape(flat),
        target_mass.reshape(flat),
    )
    outs = pl.pallas_call(
        unpack_kernel,
        out_shape=[jax.ShapeDtypeStruct(flat, F32)] * 4,
        in_specs=[whole],
        out_specs=[whole] * 4,
    )(packed)
    return tuple(out.reshape(count) for out in outs)


def solution(mesh):
    return jax.shard_map(
        functools.partial(body, mesh.shape["row"]),
        mesh=mesh,
        in_specs=(P("row", "col"), P("col", None), P("row"), P("col")),
        out_specs=(P("row"), P("col"), P("row"), P("col")),
        check_vma=False,
    )
```

```python
import functools
import math

import jax
import jax.numpy as jnp
from jax import lax
from jax.experimental import pallas as pl
from jax.experimental.pallas import tpu as pltpu
from jax.sharding import PartitionSpec as P

MESH = pl.DeviceIdType.MESH
EPSILON = 0.25
REACH = 1.0
DAMPING = 1.0 / (1.0 + EPSILON / REACH)
LOG2E = math.log2(math.e)
LN2 = math.log(2.0)
SCALE = LOG2E / EPSILON
STEP = -0.5 * DAMPING
OUT = -0.5 * DAMPING * EPSILON * LN2
LANES = 128
F32 = jnp.float32
BF16 = jnp.bfloat16


def split3(value):
    high = value.astype(BF16).astype(F32)
    rest = value - high
    middle = rest.astype(BF16).astype(F32)
    low = (rest - middle).astype(BF16).astype(F32)
    return high, middle, low


def lane_block(k):
    return pl.ds(pl.multiple_of(k * LANES, LANES), LANES)


def side_rows(first, second, count):
    index = lax.broadcasted_iota(jnp.int32, (count, LANES), 0)
    rows = jnp.zeros((count, LANES), F32)
    for position, piece in enumerate(tuple(first) + tuple(second)):
        rows = jnp.where(index == position, piece, rows)
    return rows


def half_norm(points):
    return 0.5 * jnp.sum(points * points, axis=0, keepdims=True)


def right_block(b_ref, k, points):
    channels = points.shape[0]
    block = lane_block(k)
    narrow = points.astype(BF16)
    for copy in range(3):
        b_ref[copy * channels : (copy + 1) * channels, block] = narrow
    one = jnp.ones((1, LANES), F32)
    rows = side_rows((one, one, one), split3(-SCALE * half_norm(points)), 256 - 3 * channels)
    b_ref[3 * channels : 256, block] = rows.astype(BF16)


def left_block(a_ref, k, points, weight, whole):
    channels = points.shape[0]
    rows = pl.ds(pl.multiple_of(k * LANES, LANES), LANES)
    high, middle, low = split3(SCALE * points)
    if whole:
        a_ref[rows, 0:LANES] = jnp.concatenate([high, middle], axis=0).T.astype(BF16)
    one = jnp.ones((1, LANES), F32)
    side = side_rows(split3(weight - SCALE * half_norm(points)), (one, one, one), LANES - channels)
    a_ref[rows, LANES : 2 * LANES] = jnp.concatenate([low, side], axis=0).T.astype(BF16)


CHUNK = 256
LSE_WIDE = 1024
LSE_CHUNK = 128
KERNEL_WIDE = 1024
SUM_UNROLL = 4
UNROLL = 8


def fold(value, op):
    return op(value.reshape(value.shape[0] // 8, 8, value.shape[1]), axis=0)


def emit(out_ref, j, row, wide):
    per = wide // LANES
    for t in range(per):
        piece = row[:, t * LANES : (t + 1) * LANES]
        out_ref[pl.ds(j * per + t, 1), :] = piece


def lse_pass(a_ref, b_ref, held, out_ref):
    wide = held[0].shape[1]
    chunks = a_ref.shape[0] // LSE_CHUNK

    def column(j, carry):
        columns = pl.ds(pl.multiple_of(j * wide, wide), wide)
        right = b_ref[:, columns]

        def product(i):
            left = a_ref[i * LSE_CHUNK : (i + 1) * LSE_CHUNK, :]
            part = jnp.dot(left, right, preferred_element_type=F32)
            held[i % 2][...] = part
            return fold(part, jnp.max)

        top = jnp.full((8, wide), -1e30, F32)
        total = jnp.zeros((8, wide), F32)
        peak = product(0)
        for i in range(chunks):
            fresh = jnp.maximum(top, peak)
            if i + 1 < chunks:
                peak = product(i + 1)
            part = held[i % 2][...].reshape(LSE_CHUNK // 8, 8, wide)
            total = total * jnp.exp2(top - fresh) + jnp.sum(jnp.exp2(part - fresh[None]), axis=0)
            top = fresh
        peak = jnp.max(top, axis=0, keepdims=True)
        total = jnp.sum(total * jnp.exp2(top - peak), axis=0, keepdims=True)
        emit(out_ref, j, peak + jnp.log2(total), wide)
        return carry

    lax.fori_loop(0, b_ref.shape[1] // wide, column, 0)


def kernel_pass(a_ref, b_ref, k_ref, out_ref):
    wide = min(KERNEL_WIDE, b_ref.shape[1])
    chunks = a_ref.shape[0] // CHUNK

    def step(j, carry):
        columns = pl.ds(pl.multiple_of(j * wide, wide), wide)
        right = b_ref[:, columns]
        total = jnp.zeros((8, wide), F32)
        for i in range(chunks):
            rows = slice(i * CHUNK, (i + 1) * CHUNK)
            part = jnp.exp2(jnp.dot(a_ref[rows, :], right, preferred_element_type=F32))
            k_ref[rows, columns] = part
            total = total + fold(part, jnp.sum)
        emit(out_ref, j, jnp.sum(total, axis=0, keepdims=True), wide)
        return carry

    lax.fori_loop(0, b_ref.shape[1] // wide, step, 0)


def weighted_pass(q_ref, k_ref, out_ref):
    def step(i, carry):
        rows = lane_block(i)
        total = jnp.zeros((LANES, LANES), F32)
        for t in range(k_ref.shape[1] // LANES):
            total = total + k_ref[rows, t * LANES : (t + 1) * LANES] * q_ref[t : t + 1, :]
        out_ref[pl.ds(i, 1), :] = jnp.sum(fold(total.T, jnp.sum), axis=0, keepdims=True)
        return carry

    lax.fori_loop(0, k_ref.shape[0] // LANES, step, 0, unroll=SUM_UNROLL)


CR, CC, ST, SS = 0, 1, 2, 3
GX, GT, GS = 0, 1, 2
OPS = 3 + 8 + 4


def body_kernel(
    size,
    xs_hbm,
    yt_hbm,
    ms_hbm,
    mt_hbm,
    out_ref,
    xs_ref,
    yt_ref,
    ms_ref,
    mt_ref,
    xg,
    tg,
    sg,
    x32,
    ax,
    ay,
    bx,
    by,
    bs,
    bt,
    ks,
    kt,
    m0,
    m1,
    weights,
    lms,
    lmt,
    parts,
    inboxes,
    logs,
    own_logs,
    masses,
    local_sems,
    send_sems,
    recv_sems,
):
    row, col = lax.axis_index("row"), lax.axis_index("col")
    place = {"row": row, "col": col}

    def peer(axis, k):
        return lax.rem(place[axis] + k, size)

    barrier = pltpu.get_barrier_semaphore()

    def greet(k, carry):
        for axis in ("col", "row"):
            pl.semaphore_signal(
                barrier, inc=1, device_id={axis: peer(axis, k)}, device_id_type=MESH
            )
        return carry

    lax.fori_loop(1, size, greet, 0)

    loads = [
        pltpu.make_async_copy(source, target, local_sems.at[index])
        for index, (source, target) in enumerate(
            ((yt_hbm, yt_ref), (mt_hbm, mt_ref), (ms_hbm, ms_ref), (xs_hbm, xs_ref))
        )
    ]
    for load in loads:
        load.start()

    def send_all(op, axis, source, target):
        slot = target.at[place[axis]]

        def one(i, carry):
            half = (i + 1) // 2
            other = peer(axis, size // 2 + half * (2 * lax.rem(i, 2) - 1))
            pltpu.make_async_remote_copy(
                src_ref=source,
                dst_ref=slot,
                send_sem=send_sems.at[op],
                recv_sem=recv_sems.at[op],
                device_id={axis: other},
                device_id_type=MESH,
            ).start()
            return carry

        lax.fori_loop(0, size - 1, one, 0)

    def wait_all(sems, op, target):
        others = target.at[pl.ds(0, size - 1)]
        pltpu.make_async_copy(others, others, sems.at[op]).wait()

    def blocks(step):
        def run(k, carry):
            step(k)
            return carry

        lax.fori_loop(0, size, run, 0, unroll=UNROLL)

    for load in loads:
        load.wait()
    log_mass_x = jnp.log2(ms_ref[...].astype(F32))
    log_mass_y = jnp.log2(mt_ref[...].astype(F32))
    lms[...] = log_mass_x
    lmt[...] = log_mass_y

    def prepare_y(k):
        points = yt_ref[:, lane_block(k)].astype(F32)
        right_block(by, k, points)
        left_block(ay, k, points, lmt[pl.ds(k, 1), :], True)

    blocks(prepare_y)
    tg[col] = yt_ref[:, lane_block(row)]
    xg[col] = xs_ref[...]

    pl.semaphore_wait(barrier, 2 * (size - 1))
    send_all(GX, "col", xs_ref, xg)
    send_all(GT, "col", yt_ref.at[:, lane_block(row)], tg)

    for which, axis, source in ((ST, "col", lmt), (SS, "row", lms)):
        box = masses.at[which - ST]
        box[place[axis]] = source[pl.ds(place["row" if axis == "col" else "col"], 1), :]
        send_all(13 + which - ST, axis, box.at[place[axis]], box)

    wait_all(recv_sems, GX, xg)
    group = xs_ref.shape[0]
    for c in range(size):
        x32[c * group : (c + 1) * group, :] = xg[c].astype(F32)

    def prepare_x(k):
        points = x32[:, lane_block(k)]
        right_block(bx, k, points)
        left_block(ax, k, points, lms[pl.ds(k, 1), :], True)

    blocks(prepare_x)
    channels = x32.shape[0]
    send_all(GS, "row", bx.at[0:channels, lane_block(col)], sg)
    sg[row] = bx[0:channels, lane_block(col)]

    AXIS = (("col", "row", "col", "row"), ("col", "row", "row", "col"))

    def op_of(it, which):
        return 3 + 4 * it + which

    def send_parts(it, which):
        axis = AXIS[it][which]
        part, inbox = parts.at[it, which], inboxes.at[it, which]
        send_all(op_of(it, which), axis, part, inbox)
        inbox[place[axis]] = part[...]

    def own_op(which):
        return 11 + which - ST

    def send_own(which):
        box, axis = own_logs.at[which - ST], AXIS[1][which]
        me = place[axis]
        box[me] = logs[which, pl.ds(place[AXIS[0][which]], 1), :]
        send_all(own_op(which), axis, box.at[me], box)

    def combine(it, which):
        inbox = inboxes.at[it, which]
        wait_all(recv_sems, op_of(it, which), inbox)
        values = inbox[...]
        if which in (CR, CC):
            top = jnp.max(values, axis=0)
            total = top + jnp.log2(jnp.sum(jnp.exp2(values - top[None]), axis=0))
        else:
            total = jnp.log2(jnp.sum(values, axis=0))
            if it == 1:
                total = total - (lms if which == SS else lmt)[...]
        if it == 0:
            logs[which] = total
            if which in (ST, SS):
                send_own(which)
        elif which in (CR, CC):
            out_ref[which] = (0.5 * OUT) * logs[which] + OUT * total
        else:
            box = own_logs.at[which - ST]
            wait_all(recv_sems, own_op(which), box)
            for k in range(size):
                out_ref[which, k : k + 1, :] = (0.5 * OUT) * box[k] + OUT * total[k : k + 1, :]

    def prepare_right(b_ref, inbox):
        blocks(lambda k: right_block(b_ref, k, inbox[k].astype(F32)))

    def reweight(a_ref, b_ref, mass, which):
        def step(k):
            points = b_ref[0:channels, lane_block(k)].astype(F32)
            one = pl.ds(k, 1)
            left_block(a_ref, k, points, mass[one, :] + STEP * logs[which, one, :], False)

        blocks(step)

    def row_sums(k_ref, which):
        box = masses.at[which - ST]
        wait_all(recv_sems, 13 + which - ST, box)
        for k in range(size):
            weights[k : k + 1, :] = jnp.exp2(box[k] + STEP * logs[which, k : k + 1, :])
        weighted_pass(weights, k_ref, parts.at[1, which])

    held = (m0, m1)
    lse_pass(ax, by, held, parts.at[0, CC])
    send_parts(0, CC)
    lse_pass(ay, bx, held, parts.at[0, CR])
    send_parts(0, CR)
    wait_all(recv_sems, GT, tg)
    prepare_right(bt, tg)
    kernel_pass(ay, bt, kt, parts.at[0, ST])
    send_parts(0, ST)
    wait_all(recv_sems, GS, sg)
    prepare_right(bs, sg)
    kernel_pass(ax, bs, ks, parts.at[0, SS])
    send_parts(0, SS)
    combine(0, CC)
    reweight(ay, by, lmt, CC)
    lse_pass(ay, bx, held, parts.at[1, CR])
    send_parts(1, CR)
    combine(0, SS)
    row_sums(ks, SS)
    send_parts(1, SS)
    combine(0, ST)
    row_sums(kt, ST)
    send_parts(1, ST)
    combine(0, CR)
    reweight(ax, bx, lms, CR)
    lse_pass(ax, by, held, parts.at[1, CC])
    send_parts(1, CC)
    for which in (CR, SS, ST, CC):
        combine(1, which)

    wait_all(send_sems, GX, xg)
    wait_all(send_sems, GT, tg)
    wait_all(send_sems, GS, sg)
    for which in (ST, SS):
        wait_all(send_sems, 13 + which - ST, masses.at[which - ST])
        wait_all(send_sems, own_op(which), own_logs.at[which - ST])
    for it in range(2):
        for which in range(4):
            wait_all(send_sems, op_of(it, which), inboxes.at[it, which])


def unpack_kernel(all_ref, cs_ref, ct_ref, ss_ref, st_ref):
    cs_ref[...] = all_ref[CR]
    ct_ref[...] = all_ref[CC]
    ss_ref[...] = all_ref[SS]
    st_ref[...] = all_ref[ST]


def body(size, source_desc, target_desc, source_mass, target_mass):
    count, group = source_desc.shape
    channels = target_desc.shape[1]
    flat = (size, LANES)
    whole = pl.BlockSpec(memory_space=pltpu.VMEM)
    packed = pl.pallas_call(
        functools.partial(body_kernel, size),
        out_shape=jax.ShapeDtypeStruct((4,) + flat, F32),
        in_specs=[pl.BlockSpec(memory_space=pl.ANY)] * 4,
        out_specs=whole,
        scratch_shapes=[
            pltpu.VMEM((group, count), BF16),
            pltpu.VMEM((channels, count), BF16),
            pltpu.VMEM(flat, BF16),
            pltpu.VMEM(flat, BF16),
            pltpu.VMEM((size, group, count), BF16),
            pltpu.VMEM((size, channels, LANES), BF16),
            pltpu.VMEM((size, channels, LANES), BF16),
            pltpu.VMEM((channels, count), F32),
            pltpu.VMEM((count, 256), BF16),
            pltpu.VMEM((count, 256), BF16),
            pltpu.VMEM((256, count), BF16),
            pltpu.VMEM((256, count), BF16),
            pltpu.VMEM((256, count), BF16),
            pltpu.VMEM((256, count), BF16),
            pltpu.VMEM((count, count), F32),
            pltpu.VMEM((count, count), F32),
            pltpu.VMEM((LSE_CHUNK, min(LSE_WIDE, count)), F32),
            pltpu.VMEM((LSE_CHUNK, min(LSE_WIDE, count)), F32),
            pltpu.VMEM(flat, F32),
            pltpu.VMEM(flat, F32),
            pltpu.VMEM(flat, F32),
            pltpu.VMEM((2, 4) + flat, F32),
            pltpu.VMEM((2, 4, size) + flat, F32),
            pltpu.VMEM((4,) + flat, F32),
            pltpu.VMEM((2, size, 1, LANES), F32),
            pltpu.VMEM((2, size, 1, LANES), F32),
            pltpu.SemaphoreType.DMA((4,)),
            pltpu.SemaphoreType.DMA((OPS,)),
            pltpu.SemaphoreType.DMA((OPS,)),
        ],
        compiler_params=pltpu.CompilerParams(
            collective_id=0, has_side_effects=True, vmem_limit_bytes=56 * 1024 * 1024
        ),
    )(
        source_desc.T,
        target_desc.T,
        source_mass.reshape(flat),
        target_mass.reshape(flat),
    )
    outs = pl.pallas_call(
        unpack_kernel,
        out_shape=[jax.ShapeDtypeStruct(flat, F32)] * 4,
        in_specs=[whole],
        out_specs=[whole] * 4,
    )(packed)
    return tuple(out.reshape(count) for out in outs)


def solution(mesh):
    return jax.shard_map(
        functools.partial(body, mesh.shape["row"]),
        mesh=mesh,
        in_specs=(P("row", "col"), P("col", None), P("row"), P("col")),
        out_specs=(P("row"), P("col"), P("row"), P("col")),
        check_vma=False,
    )
```

```python
import functools
import math

import jax
import jax.numpy as jnp
from jax import lax
from jax.experimental import pallas as pl
from jax.experimental.pallas import tpu as pltpu
from jax.sharding import PartitionSpec as P

MESH = pl.DeviceIdType.MESH
EPSILON = 0.25
REACH = 1.0
DAMPING = 1.0 / (1.0 + EPSILON / REACH)
LOG2E = math.log2(math.e)
LN2 = math.log(2.0)
SCALE = LOG2E / EPSILON
STEP = -0.5 * DAMPING
OUT = -0.5 * DAMPING * EPSILON * LN2
LANES = 128
F32 = jnp.float32
BF16 = jnp.bfloat16


def split3(value):
    high = value.astype(BF16).astype(F32)
    rest = value - high
    middle = rest.astype(BF16).astype(F32)
    low = (rest - middle).astype(BF16).astype(F32)
    return high, middle, low


def lane_block(k):
    return pl.ds(pl.multiple_of(k * LANES, LANES), LANES)


def side_rows(first, second, count):
    index = lax.broadcasted_iota(jnp.int32, (count, LANES), 0)
    rows = jnp.zeros((count, LANES), F32)
    for position, piece in enumerate(tuple(first) + tuple(second)):
        rows = jnp.where(index == position, piece, rows)
    return rows


def half_norm(points):
    return 0.5 * jnp.sum(points * points, axis=0, keepdims=True)


def right_block(b_ref, k, points):
    channels = points.shape[0]
    block = lane_block(k)
    narrow = points.astype(BF16)
    for copy in range(3):
        b_ref[copy * channels : (copy + 1) * channels, block] = narrow
    one = jnp.ones((1, LANES), F32)
    rows = side_rows((one, one, one), split3(-SCALE * half_norm(points)), 256 - 3 * channels)
    b_ref[3 * channels : 256, block] = rows.astype(BF16)


def left_block(a_ref, k, points, weight, whole):
    channels = points.shape[0]
    rows = pl.ds(pl.multiple_of(k * LANES, LANES), LANES)
    high, middle, low = split3(SCALE * points)
    if whole:
        a_ref[rows, 0:LANES] = jnp.concatenate([high, middle], axis=0).T.astype(BF16)
    one = jnp.ones((1, LANES), F32)
    side = side_rows(split3(weight - SCALE * half_norm(points)), (one, one, one), LANES - channels)
    a_ref[rows, LANES : 2 * LANES] = jnp.concatenate([low, side], axis=0).T.astype(BF16)


CHUNK = 256
LSE_WIDE = 1024
LSE_CHUNK = 128
KERNEL_WIDE = 1024
SUM_UNROLL = 4
UNROLL = 8


def fold(value, op):
    return op(value.reshape(value.shape[0] // 8, 8, value.shape[1]), axis=0)


def emit(out_ref, j, row, wide):
    per = wide // LANES
    for t in range(per):
        piece = row[:, t * LANES : (t + 1) * LANES]
        out_ref[pl.ds(j * per + t, 1), :] = piece


def lse_pass(a_ref, b_ref, held, out_ref, part_index=None):
    wide = held[0].shape[1]
    chunks = a_ref.shape[0] // LSE_CHUNK

    def column(j, carry):
        columns = pl.ds(pl.multiple_of(j * wide, wide), wide)
        right = b_ref[:, columns]

        def product(i):
            left = a_ref[i * LSE_CHUNK : (i + 1) * LSE_CHUNK, :]
            part = jnp.dot(left, right, preferred_element_type=F32)
            held[i % 2][...] = part
            return fold(part, jnp.max)

        top = jnp.full((8, wide), -1e30, F32)
        total = jnp.zeros((8, wide), F32)
        peak = product(0)
        for i in range(chunks):
            fresh = jnp.maximum(top, peak)
            if i + 1 < chunks:
                peak = product(i + 1)
            part = held[i % 2][...].reshape(LSE_CHUNK // 8, 8, wide)
            total = total * jnp.exp2(top - fresh) + jnp.sum(jnp.exp2(part - fresh[None]), axis=0)
            top = fresh
        peak = jnp.max(top, axis=0, keepdims=True)
        total = jnp.sum(total * jnp.exp2(top - peak), axis=0, keepdims=True)
        emit(out_ref, j, peak + jnp.log2(total), wide)
        return carry

    blocks = b_ref.shape[1] // wide
    if part_index is None:
        lax.fori_loop(0, blocks, column, 0)
    else:
        lax.fori_loop(part_index * blocks // 2, (part_index + 1) * blocks // 2, column, 0)


def kernel_pass(a_ref, b_ref, k_ref, out_ref):
    wide = min(KERNEL_WIDE, b_ref.shape[1])
    chunks = a_ref.shape[0] // CHUNK

    def step(j, carry):
        columns = pl.ds(pl.multiple_of(j * wide, wide), wide)
        right = b_ref[:, columns]
        total = jnp.zeros((8, wide), F32)
        for i in range(chunks):
            rows = slice(i * CHUNK, (i + 1) * CHUNK)
            part = jnp.exp2(jnp.dot(a_ref[rows, :], right, preferred_element_type=F32))
            k_ref[rows, columns] = part
            total = total + fold(part, jnp.sum)
        emit(out_ref, j, jnp.sum(total, axis=0, keepdims=True), wide)
        return carry

    lax.fori_loop(0, b_ref.shape[1] // wide, step, 0)


def weighted_pass(q_ref, k_ref, out_ref):
    def step(i, carry):
        rows = lane_block(i)
        total = jnp.zeros((LANES, LANES), F32)
        for t in range(k_ref.shape[1] // LANES):
            total = total + k_ref[rows, t * LANES : (t + 1) * LANES] * q_ref[t : t + 1, :]
        out_ref[pl.ds(i, 1), :] = jnp.sum(fold(total.T, jnp.sum), axis=0, keepdims=True)
        return carry

    lax.fori_loop(0, k_ref.shape[0] // LANES, step, 0, unroll=SUM_UNROLL)


CR, CC, ST, SS = 0, 1, 2, 3
GS = 0
FIRST_OP = 1
OWN_OP = FIRST_OP + 8
MASS_OP = OWN_OP + 2
HALF_OP = MASS_OP + 2
TREE_OP = HALF_OP + 1


def body_kernel(
    size,
    xs_hbm,
    yt_hbm,
    ms_hbm,
    mt_hbm,
    out_ref,
    xs_ref,
    yt_ref,
    ms_ref,
    mt_ref,
    xg,
    tg,
    sg,
    x32,
    ax,
    ay,
    bx,
    by,
    bs,
    bt,
    ks,
    kt,
    m0,
    m1,
    weights,
    lms,
    lmt,
    parts,
    inboxes,
    logs,
    own_logs,
    masses,
    local_sems,
    send_sems,
    recv_sems,
):
    row, col = lax.axis_index("row"), lax.axis_index("col")
    place = {"row": row, "col": col}

    def peer(axis, k):
        return lax.rem(place[axis] + k, size)

    barrier = pltpu.get_barrier_semaphore()

    def greet(k, carry):
        for axis in ("col", "row"):
            pl.semaphore_signal(
                barrier, inc=1, device_id={axis: peer(axis, k)}, device_id_type=MESH
            )
        return carry

    lax.fori_loop(1, size, greet, 0)

    loads = [
        pltpu.make_async_copy(source, target, local_sems.at[index])
        for index, (source, target) in enumerate(
            ((yt_hbm, yt_ref), (mt_hbm, mt_ref), (ms_hbm, ms_ref), (xs_hbm, xs_ref))
        )
    ]
    for load in loads:
        load.start()

    def send_all(op, axis, source, slot):
        def one(i, carry):
            half = (i + 1) // 2
            other = peer(axis, size // 2 + half * (2 * lax.rem(i, 2) - 1))
            pltpu.make_async_remote_copy(
                src_ref=source,
                dst_ref=slot,
                send_sem=send_sems.at[op],
                recv_sem=recv_sems.at[op],
                device_id={axis: other},
                device_id_type=MESH,
            ).start()
            return carry

        lax.fori_loop(0, size - 1, one, 0)

    inner = math.isqrt(size)
    outer = size // inner
    at_outer, at_inner = col // inner, lax.rem(col, inner)

    def spot(out_index, in_index):
        return in_index * outer + out_index

    def tree_send(op, box, slot, device):
        pltpu.make_async_remote_copy(
            src_ref=box.at[slot],
            dst_ref=box.at[slot],
            send_sem=send_sems.at[op],
            recv_sem=recv_sems.at[op],
            device_id={"col": device},
            device_id_type=MESH,
        ).start()

    class Tree:
        def __init__(self, first_op, box):
            self.first_op, self.box = first_op, box

        def start(self):
            slot = spot(at_outer, at_inner)
            for k in sorted(range(1, outer), key=lambda k: -min(k, outer - k)):
                other = lax.rem(at_outer + k, outer)
                tree_send(self.first_op + k, self.box, slot, other * inner + at_inner)
            self.spread(slot)

        def spread(self, slot):
            for k in range(1, inner):
                other = lax.rem(at_inner + k, inner)
                tree_send(self.first_op, self.box, slot, at_outer * inner + other)

        def forward(self, k):
            slot = spot(lax.rem(at_outer + outer - k, outer), at_inner)
            wait_one(recv_sems, self.first_op + k, self.box.at[slot])
            self.spread(slot)

        def wait(self, sems):
            wait_one(sems, self.first_op, self.box.at[pl.ds(0, outer * (inner - 1))])

        def wait_sends(self):
            self.wait(send_sems)
            for k in range(1, outer):
                wait_one(send_sems, self.first_op + k, self.box.at[0])

    def wait_one(sems, op, target):
        pltpu.make_async_copy(target, target, sems.at[op]).wait()

    def wait_all(sems, op, target):
        wait_one(sems, op, target.at[pl.ds(0, size - 1)])

    def blocks(step):
        def run(k, carry):
            step(k)
            return carry

        lax.fori_loop(0, size, run, 0, unroll=UNROLL)

    for load in loads:
        load.wait()
    log_mass_x = jnp.log2(ms_ref[...].astype(F32))
    log_mass_y = jnp.log2(mt_ref[...].astype(F32))
    lms[...] = log_mass_x
    lmt[...] = log_mass_y

    def prepare_y(k):
        points = yt_ref[:, lane_block(k)].astype(F32)
        right_block(by, k, points)
        left_block(ay, k, points, lmt[pl.ds(k, 1), :], True)

    blocks(prepare_y)
    mine = spot(at_outer, at_inner)
    tg[mine] = yt_ref[:, lane_block(row)]
    xg[mine] = xs_ref[...]
    slot_of = {ST: mine, SS: row}
    piece_of = {ST: row, SS: col}
    for which, source in ((ST, lmt), (SS, lms)):
        masses[which - ST, slot_of[which]] = source[pl.ds(piece_of[which], 1), :]

    pl.semaphore_wait(barrier, 2 * (size - 1))
    tree_x, tree_t = Tree(TREE_OP, xg), Tree(TREE_OP + outer, tg)
    tree_x.start()
    tree_t.start()
    for k in sorted(range(1, outer), key=lambda k: min(k, outer - k)):
        tree_x.forward(k)
        tree_t.forward(k)
    for which, axis in ((ST, "col"), (SS, "row")):
        slot = masses.at[which - ST, slot_of[which]]
        send_all(MASS_OP + which - ST, axis, slot, slot)

    tree_x.wait(recv_sems)
    group = xs_ref.shape[0]
    for c in range(size):
        block = xg[spot(c // inner, c % inner)]
        x32[c * group : (c + 1) * group, :] = block.astype(F32)

    def prepare_x(k):
        points = x32[:, lane_block(k)]
        right_block(bx, k, points)
        left_block(ax, k, points, lms[pl.ds(k, 1), :], True)

    blocks(prepare_x)
    channels = x32.shape[0]
    send_all(GS, "row", bx.at[0:channels, lane_block(col)], sg.at[row])
    sg[row] = bx[0:channels, lane_block(col)]

    AXIS = (("col", "row", "col", "row"), ("col", "row", "row", "col"))

    def op_of(it, which):
        return FIRST_OP + 4 * it + which

    def send_parts(it, which):
        axis = AXIS[it][which]
        part, inbox = parts.at[it, which], inboxes.at[it, which]
        me = place[axis]
        send_all(op_of(it, which), axis, part, inbox.at[me])
        inbox[me] = part[...]

    def own_op(which):
        return OWN_OP + which - ST

    def send_own(which):
        box, axis = own_logs.at[which - ST], AXIS[1][which]
        me = place[axis]
        box[me] = logs[which, pl.ds(slot_of[which], 1), :]
        send_all(own_op(which), axis, box.at[me], box.at[me])

    half = size // 2

    def send_half(part_index):
        rows = pl.ds(part_index * half, half)
        part, slot = parts.at[1, CC, rows], inboxes.at[1, CC, row, rows]
        send_all(op_of(1, CC) if part_index == 0 else HALF_OP, "row", part, slot)
        if part_index == 1:
            inboxes[1, CC, row] = parts[1, CC]

    def wait_parts(sems, it, which):
        inbox = inboxes.at[it, which]
        if (it, which) == (1, CC):
            some = inbox.at[pl.ds(0, size - 1), pl.ds(0, half)]
            wait_one(sems, op_of(it, which), some)
            wait_one(sems, HALF_OP, some)
        else:
            wait_all(sems, op_of(it, which), inbox)

    def combine(it, which):
        inbox = inboxes.at[it, which]
        wait_parts(recv_sems, it, which)
        values = inbox[...]
        if which in (CR, CC):
            top = jnp.max(values, axis=0)
            total = top + jnp.log2(jnp.sum(jnp.exp2(values - top[None]), axis=0))
        else:
            total = jnp.log2(jnp.sum(values, axis=0))
            if it == 1:
                total = total - (lms if which == SS else lmt)[...]
        if it == 0:
            logs[which] = total
            if which in (ST, SS):
                send_own(which)
        elif which in (CR, CC):
            out_ref[which] = (0.5 * OUT) * logs[which] + OUT * total
        else:
            box = own_logs.at[which - ST]
            wait_all(recv_sems, own_op(which), box)
            for k in range(size):
                out_ref[which, k : k + 1, :] = (0.5 * OUT) * box[k] + OUT * total[k : k + 1, :]

    def prepare_right(b_ref, inbox):
        blocks(lambda k: right_block(b_ref, k, inbox[k].astype(F32)))

    def reweight(a_ref, b_ref, mass, which):
        def step(k):
            points = b_ref[0:channels, lane_block(k)].astype(F32)
            one = pl.ds(k, 1)
            left_block(a_ref, k, points, mass[one, :] + STEP * logs[which, one, :], False)

        blocks(step)

    def row_sums(k_ref, which):
        box = masses.at[which - ST]
        wait_all(recv_sems, MASS_OP + which - ST, box)
        for k in range(size):
            weights[k : k + 1, :] = jnp.exp2(box[k] + STEP * logs[which, k : k + 1, :])
        weighted_pass(weights, k_ref, parts.at[1, which])

    held = (m0, m1)
    lse_pass(ax, by, held, parts.at[0, CC])
    send_parts(0, CC)
    tree_t.wait(recv_sems)
    prepare_right(bt, tg)
    kernel_pass(ay, bt, kt, parts.at[0, ST])
    send_parts(0, ST)
    lse_pass(ay, bx, held, parts.at[0, CR])
    send_parts(0, CR)
    wait_all(recv_sems, GS, sg)
    prepare_right(bs, sg)
    kernel_pass(ax, bs, ks, parts.at[0, SS])
    send_parts(0, SS)
    combine(0, CC)
    reweight(ay, by, lmt, CC)
    lse_pass(ay, bx, held, parts.at[1, CR])
    send_parts(1, CR)
    combine(0, SS)
    row_sums(ks, SS)
    send_parts(1, SS)
    combine(0, ST)
    row_sums(kt, ST)
    send_parts(1, ST)
    combine(0, CR)
    reweight(ax, bx, lms, CR)
    for part_index in range(2):
        lse_pass(ax, by, held, parts.at[1, CC], part_index)
        send_half(part_index)
    for which in (CR, SS, ST, CC):
        combine(1, which)

    tree_x.wait_sends()
    tree_t.wait_sends()
    wait_all(send_sems, GS, sg)
    for which in (ST, SS):
        wait_all(send_sems, MASS_OP + which - ST, masses.at[which - ST])
        wait_all(send_sems, own_op(which), own_logs.at[which - ST])
    for it in range(2):
        for which in range(4):
            wait_parts(send_sems, it, which)


def unpack_kernel(all_ref, cs_ref, ct_ref, ss_ref, st_ref):
    cs_ref[...] = all_ref[CR]
    ct_ref[...] = all_ref[CC]
    ss_ref[...] = all_ref[SS]
    st_ref[...] = all_ref[ST]


def body(size, source_desc, target_desc, source_mass, target_mass):
    count, group = source_desc.shape
    channels = target_desc.shape[1]
    flat = (size, LANES)
    ops = TREE_OP + 2 * (size // math.isqrt(size))
    wide = min(LSE_WIDE, count // 2)
    whole = pl.BlockSpec(memory_space=pltpu.VMEM)
    packed = pl.pallas_call(
        functools.partial(body_kernel, size),
        out_shape=jax.ShapeDtypeStruct((4,) + flat, F32),
        in_specs=[pl.BlockSpec(memory_space=pl.ANY)] * 4,
        out_specs=whole,
        scratch_shapes=[
            pltpu.VMEM((group, count), BF16),
            pltpu.VMEM((channels, count), BF16),
            pltpu.VMEM(flat, BF16),
            pltpu.VMEM(flat, BF16),
            pltpu.VMEM((size, group, count), BF16),
            pltpu.VMEM((size, channels, LANES), BF16),
            pltpu.VMEM((size, channels, LANES), BF16),
            pltpu.VMEM((channels, count), F32),
            pltpu.VMEM((count, 256), BF16),
            pltpu.VMEM((count, 256), BF16),
            pltpu.VMEM((256, count), BF16),
            pltpu.VMEM((256, count), BF16),
            pltpu.VMEM((256, count), BF16),
            pltpu.VMEM((256, count), BF16),
            pltpu.VMEM((count, count), F32),
            pltpu.VMEM((count, count), F32),
            pltpu.VMEM((LSE_CHUNK, wide), F32),
            pltpu.VMEM((LSE_CHUNK, wide), F32),
            pltpu.VMEM(flat, F32),
            pltpu.VMEM(flat, F32),
            pltpu.VMEM(flat, F32),
            pltpu.VMEM((2, 4) + flat, F32),
            pltpu.VMEM((2, 4, size) + flat, F32),
            pltpu.VMEM((4,) + flat, F32),
            pltpu.VMEM((2, size, 1, LANES), F32),
            pltpu.VMEM((2, size, 1, LANES), F32),
            pltpu.SemaphoreType.DMA((4,)),
            pltpu.SemaphoreType.DMA((ops,)),
            pltpu.SemaphoreType.DMA((ops,)),
        ],
        compiler_params=pltpu.CompilerParams(
            collective_id=0, has_side_effects=True, vmem_limit_bytes=56 * 1024 * 1024
        ),
    )(
        source_desc.T,
        target_desc.T,
        source_mass.reshape(flat),
        target_mass.reshape(flat),
    )
    outs = pl.pallas_call(
        unpack_kernel,
        out_shape=[jax.ShapeDtypeStruct(flat, F32)] * 4,
        in_specs=[whole],
        out_specs=[whole] * 4,
    )(packed)
    return tuple(out.reshape(count) for out in outs)


def solution(mesh):
    return jax.shard_map(
        functools.partial(body, mesh.shape["row"]),
        mesh=mesh,
        in_specs=(P("row", "col"), P("col", None), P("row"), P("col")),
        out_specs=(P("row"), P("col"), P("row"), P("col")),
        check_vma=False,
    )
```

```python
import functools
import math

import jax
import jax.numpy as jnp
from jax import lax
from jax.experimental import pallas as pl
from jax.experimental.pallas import tpu as pltpu
from jax.sharding import PartitionSpec as P

MESH = pl.DeviceIdType.MESH
EPSILON = 0.25
REACH = 1.0
DAMPING = 1.0 / (1.0 + EPSILON / REACH)
LOG2E = math.log2(math.e)
LN2 = math.log(2.0)
SCALE = LOG2E / EPSILON
STEP = -0.5 * DAMPING
OUT = -0.5 * DAMPING * EPSILON * LN2
LANES = 128
F32 = jnp.float32
BF16 = jnp.bfloat16


def split3(value):
    high = value.astype(BF16).astype(F32)
    rest = value - high
    middle = rest.astype(BF16).astype(F32)
    low = (rest - middle).astype(BF16).astype(F32)
    return high, middle, low


def lane_block(k):
    return pl.ds(pl.multiple_of(k * LANES, LANES), LANES)


def side_rows(first, second, count):
    index = lax.broadcasted_iota(jnp.int32, (count, LANES), 0)
    rows = jnp.zeros((count, LANES), F32)
    for position, piece in enumerate(tuple(first) + tuple(second)):
        rows = jnp.where(index == position, piece, rows)
    return rows


def half_norm(points):
    return 0.5 * jnp.sum(points * points, axis=0, keepdims=True)


def right_block(b_ref, k, points):
    channels = points.shape[0]
    block = lane_block(k)
    narrow = points.astype(BF16)
    for copy in range(3):
        b_ref[copy * channels : (copy + 1) * channels, block] = narrow
    one = jnp.ones((1, LANES), F32)
    rows = side_rows((one, one, one), split3(-SCALE * half_norm(points)), 256 - 3 * channels)
    b_ref[3 * channels : 256, block] = rows.astype(BF16)


def left_block(a_ref, k, points, weight, whole):
    channels = points.shape[0]
    rows = pl.ds(pl.multiple_of(k * LANES, LANES), LANES)
    high, middle, low = split3(SCALE * points)
    if whole:
        a_ref[rows, 0:LANES] = jnp.concatenate([high, middle], axis=0).T.astype(BF16)
    one = jnp.ones((1, LANES), F32)
    side = side_rows(split3(weight - SCALE * half_norm(points)), (one, one, one), LANES - channels)
    a_ref[rows, LANES : 2 * LANES] = jnp.concatenate([low, side], axis=0).T.astype(BF16)


CHUNK = 256
LSE_WIDE = 1024
LSE_CHUNK = 128
KERNEL_WIDE = 1024
SUM_UNROLL = 4
SEND_UNROLL = 5
UNROLL = 8


def fold(value, op):
    return op(value.reshape(value.shape[0] // 8, 8, value.shape[1]), axis=0)


def emit(out_ref, j, row, wide):
    per = wide // LANES
    for t in range(per):
        piece = row[:, t * LANES : (t + 1) * LANES]
        out_ref[pl.ds(j * per + t, 1), :] = piece


def lse_pass(a_ref, b_ref, held, out_ref, part_index=None):
    count = b_ref.shape[1]
    wide = min(LSE_WIDE, count if part_index is None else count // 2)
    chunks = a_ref.shape[0] // LSE_CHUNK

    def column(j, carry):
        columns = pl.ds(pl.multiple_of(j * wide, wide), wide)
        right = b_ref[:, columns]

        def product(i):
            left = a_ref[i * LSE_CHUNK : (i + 1) * LSE_CHUNK, :]
            part = jnp.dot(left, right, preferred_element_type=F32)
            held[i % 2][:, 0:wide] = part
            return fold(part, jnp.max)

        top = jnp.full((8, wide), -1e30, F32)
        total = jnp.zeros((8, wide), F32)
        peak = product(0)
        for i in range(chunks):
            fresh = jnp.maximum(top, peak)
            if i + 1 < chunks:
                peak = product(i + 1)
            part = held[i % 2][:, 0:wide].reshape(LSE_CHUNK // 8, 8, wide)
            total = total * jnp.exp2(top - fresh) + jnp.sum(jnp.exp2(part - fresh[None]), axis=0)
            top = fresh
        peak = jnp.max(top, axis=0, keepdims=True)
        total = jnp.sum(total * jnp.exp2(top - peak), axis=0, keepdims=True)
        emit(out_ref, j, peak + jnp.log2(total), wide)
        return carry

    blocks = b_ref.shape[1] // wide
    if part_index is None:
        lax.fori_loop(0, blocks, column, 0)
    else:
        lax.fori_loop(part_index * blocks // 2, (part_index + 1) * blocks // 2, column, 0)


def kernel_pass(a_ref, b_ref, k_ref, out_ref):
    wide = min(KERNEL_WIDE, b_ref.shape[1])
    chunks = a_ref.shape[0] // CHUNK

    def step(j, carry):
        columns = pl.ds(pl.multiple_of(j * wide, wide), wide)
        right = b_ref[:, columns]
        total = jnp.zeros((8, wide), F32)
        for i in range(chunks):
            rows = slice(i * CHUNK, (i + 1) * CHUNK)
            part = jnp.exp2(jnp.dot(a_ref[rows, :], right, preferred_element_type=F32))
            k_ref[rows, columns] = part
            total = total + fold(part, jnp.sum)
        emit(out_ref, j, jnp.sum(total, axis=0, keepdims=True), wide)
        return carry

    lax.fori_loop(0, b_ref.shape[1] // wide, step, 0)


def weighted_pass(q_ref, k_ref, out_ref):
    def step(i, carry):
        rows = lane_block(i)
        total = jnp.zeros((LANES, LANES), F32)
        for t in range(k_ref.shape[1] // LANES):
            total = total + k_ref[rows, t * LANES : (t + 1) * LANES] * q_ref[t : t + 1, :]
        out_ref[pl.ds(i, 1), :] = jnp.sum(fold(total.T, jnp.sum), axis=0, keepdims=True)
        return carry

    lax.fori_loop(0, k_ref.shape[0] // LANES, step, 0, unroll=SUM_UNROLL)


CR, CC, ST, SS = 0, 1, 2, 3
GS = 0
FIRST_OP = 1
OWN_OP = FIRST_OP + 8
MASS_OP = OWN_OP + 2
HALF_OP = MASS_OP + 2
TREE_OP = HALF_OP + 1


def body_kernel(
    size,
    xs_hbm,
    yt_hbm,
    ms_hbm,
    mt_hbm,
    out_ref,
    xs_ref,
    yt_ref,
    ms_ref,
    mt_ref,
    xg,
    tg,
    sg,
    x32,
    ax,
    ay,
    bx,
    by,
    bs,
    bt,
    ks,
    kt,
    m0,
    m1,
    weights,
    lms,
    lmt,
    parts,
    inboxes,
    logs,
    own_logs,
    masses,
    local_sems,
    send_sems,
    recv_sems,
):
    row, col = lax.axis_index("row"), lax.axis_index("col")
    place = {"row": row, "col": col}

    def peer(axis, k):
        return lax.rem(place[axis] + k, size)

    barrier = pltpu.get_barrier_semaphore()

    def greet(k, carry):
        for axis in ("col", "row"):
            pl.semaphore_signal(
                barrier, inc=1, device_id={axis: peer(axis, k)}, device_id_type=MESH
            )
        return carry

    lax.fori_loop(1, size, greet, 0)

    loads = [
        pltpu.make_async_copy(source, target, local_sems.at[index])
        for index, (source, target) in enumerate(
            ((yt_hbm, yt_ref), (mt_hbm, mt_ref), (ms_hbm, ms_ref), (xs_hbm, xs_ref))
        )
    ]
    for load in loads:
        load.start()

    def send_all(op, axis, source, slot):
        def one(i, carry):
            half = (i + 1) // 2
            other = peer(axis, size // 2 + half * (2 * lax.rem(i, 2) - 1))
            pltpu.make_async_remote_copy(
                src_ref=source,
                dst_ref=slot,
                send_sem=send_sems.at[op],
                recv_sem=recv_sems.at[op],
                device_id={axis: other},
                device_id_type=MESH,
            ).start()
            return carry

        lax.fori_loop(0, size - 1, one, 0, unroll=SEND_UNROLL)

    inner = math.isqrt(size)
    outer = size // inner
    at_outer, at_inner = col // inner, lax.rem(col, inner)

    def spot(out_index, in_index):
        return in_index * outer + out_index

    def tree_send(op, box, slot, device):
        pltpu.make_async_remote_copy(
            src_ref=box.at[slot],
            dst_ref=box.at[slot],
            send_sem=send_sems.at[op],
            recv_sem=recv_sems.at[op],
            device_id={"col": device},
            device_id_type=MESH,
        ).start()

    class Tree:
        def __init__(self, first_op, box):
            self.first_op, self.box = first_op, box

        def start(self):
            slot = spot(at_outer, at_inner)
            for k in sorted(range(1, outer), key=lambda k: -min(k, outer - k)):
                other = lax.rem(at_outer + k, outer)
                tree_send(self.first_op + k, self.box, slot, other * inner + at_inner)
            self.spread(slot)

        def spread(self, slot):
            for k in range(1, inner):
                other = lax.rem(at_inner + k, inner)
                tree_send(self.first_op, self.box, slot, at_outer * inner + other)

        def forward(self, k):
            slot = spot(lax.rem(at_outer + outer - k, outer), at_inner)
            wait_one(recv_sems, self.first_op + k, self.box.at[slot])
            self.spread(slot)

        def wait(self, sems):
            wait_one(sems, self.first_op, self.box.at[pl.ds(0, outer * (inner - 1))])

        def wait_sends(self):
            self.wait(send_sems)
            for k in range(1, outer):
                wait_one(send_sems, self.first_op + k, self.box.at[0])

    def wait_one(sems, op, target):
        pltpu.make_async_copy(target, target, sems.at[op]).wait()

    def wait_all(sems, op, target):
        wait_one(sems, op, target.at[pl.ds(0, size - 1)])

    def blocks(step):
        def run(k, carry):
            step(k)
            return carry

        lax.fori_loop(0, size, run, 0, unroll=UNROLL)

    for load in loads:
        load.wait()
    log_mass_x = jnp.log2(ms_ref[...].astype(F32))
    log_mass_y = jnp.log2(mt_ref[...].astype(F32))
    lms[...] = log_mass_x
    lmt[...] = log_mass_y

    def prepare_y(k):
        points = yt_ref[:, lane_block(k)].astype(F32)
        right_block(by, k, points)
        left_block(ay, k, points, lmt[pl.ds(k, 1), :], True)

    blocks(prepare_y)
    mine = spot(at_outer, at_inner)
    tg[mine] = yt_ref[:, lane_block(row)]
    xg[mine] = xs_ref[...]
    slot_of = {ST: mine, SS: row}
    piece_of = {ST: row, SS: col}
    for which, source in ((ST, lmt), (SS, lms)):
        masses[which - ST, slot_of[which]] = source[pl.ds(piece_of[which], 1), :]

    pl.semaphore_wait(barrier, 2 * (size - 1))
    tree_x, tree_t = Tree(TREE_OP, xg), Tree(TREE_OP + outer, tg)
    by_distance = sorted(range(1, outer), key=lambda k: min(k, outer - k))
    tree_x.start()
    for k in by_distance:
        tree_x.forward(k)
    tree_t.start()
    for which, axis in ((ST, "col"), (SS, "row")):
        slot = masses.at[which - ST, slot_of[which]]
        send_all(MASS_OP + which - ST, axis, slot, slot)

    tree_x.wait(recv_sems)
    group = xs_ref.shape[0]
    for c in range(size):
        block = xg[spot(c // inner, c % inner)]
        x32[c * group : (c + 1) * group, :] = block.astype(F32)

    def prepare_x(k):
        points = x32[:, lane_block(k)]
        right_block(bx, k, points)
        left_block(ax, k, points, lms[pl.ds(k, 1), :], True)

    blocks(prepare_x)
    channels = x32.shape[0]
    send_all(GS, "row", bx.at[0:channels, lane_block(col)], sg.at[row])
    sg[row] = bx[0:channels, lane_block(col)]

    AXIS = (("col", "row", "col", "row"), ("col", "row", "row", "col"))

    def op_of(it, which):
        return FIRST_OP + 4 * it + which

    def send_parts(it, which):
        axis = AXIS[it][which]
        part, inbox = parts.at[it, which], inboxes.at[it, which]
        me = place[axis]
        send_all(op_of(it, which), axis, part, inbox.at[me])
        inbox[me] = part[...]

    def own_op(which):
        return OWN_OP + which - ST

    def send_own(which):
        box, axis = own_logs.at[which - ST], AXIS[1][which]
        me = place[axis]
        box[me] = logs[which, pl.ds(slot_of[which], 1), :]
        send_all(own_op(which), axis, box.at[me], box.at[me])

    half = size // 2

    def send_half(part_index):
        rows = pl.ds(part_index * half, half)
        part, slot = parts.at[1, CC, rows], inboxes.at[1, CC, row, rows]
        send_all(op_of(1, CC) if part_index == 0 else HALF_OP, "row", part, slot)
        if part_index == 1:
            inboxes[1, CC, row] = parts[1, CC]

    def wait_parts(sems, it, which):
        inbox = inboxes.at[it, which]
        if (it, which) == (1, CC):
            some = inbox.at[pl.ds(0, size - 1), pl.ds(0, half)]
            wait_one(sems, op_of(it, which), some)
            wait_one(sems, HALF_OP, some)
        else:
            wait_all(sems, op_of(it, which), inbox)

    def combine(it, which):
        inbox = inboxes.at[it, which]
        wait_parts(recv_sems, it, which)
        values = inbox[...]
        if which in (CR, CC):
            top = jnp.max(values, axis=0)
            total = top + jnp.log2(jnp.sum(jnp.exp2(values - top[None]), axis=0))
        else:
            total = jnp.log2(jnp.sum(values, axis=0))
            if it == 1:
                total = total - (lms if which == SS else lmt)[...]
        if it == 0:
            logs[which] = total
            if which in (ST, SS):
                send_own(which)
        elif which in (CR, CC):
            out_ref[which] = (0.5 * OUT) * logs[which] + OUT * total
        else:
            box = own_logs.at[which - ST]
            wait_all(recv_sems, own_op(which), box)
            for k in range(size):
                out_ref[which, k : k + 1, :] = (0.5 * OUT) * box[k] + OUT * total[k : k + 1, :]

    def prepare_right(b_ref, inbox):
        blocks(lambda k: right_block(b_ref, k, inbox[k].astype(F32)))

    def reweight(a_ref, b_ref, mass, which):
        def step(k):
            points = b_ref[0:channels, lane_block(k)].astype(F32)
            one = pl.ds(k, 1)
            left_block(a_ref, k, points, mass[one, :] + STEP * logs[which, one, :], False)

        blocks(step)

    def row_sums(k_ref, which):
        box = masses.at[which - ST]
        wait_all(recv_sems, MASS_OP + which - ST, box)
        for k in range(size):
            weights[k : k + 1, :] = jnp.exp2(box[k] + STEP * logs[which, k : k + 1, :])
        weighted_pass(weights, k_ref, parts.at[1, which])

    held = (m0, m1)
    lse_pass(ax, by, held, parts.at[0, CC])
    send_parts(0, CC)
    for k in by_distance:
        tree_t.forward(k)
    lse_pass(ay, bx, held, parts.at[0, CR])
    send_parts(0, CR)
    tree_t.wait(recv_sems)
    prepare_right(bt, tg)
    kernel_pass(ay, bt, kt, parts.at[0, ST])
    send_parts(0, ST)
    wait_all(recv_sems, GS, sg)
    prepare_right(bs, sg)
    kernel_pass(ax, bs, ks, parts.at[0, SS])
    send_parts(0, SS)
    combine(0, CC)
    reweight(ay, by, lmt, CC)
    lse_pass(ay, bx, held, parts.at[1, CR])
    send_parts(1, CR)
    combine(0, ST)
    row_sums(kt, ST)
    send_parts(1, ST)
    combine(0, SS)
    row_sums(ks, SS)
    send_parts(1, SS)
    combine(0, CR)
    reweight(ax, bx, lms, CR)
    for part_index in range(2):
        lse_pass(ax, by, held, parts.at[1, CC], part_index)
        send_half(part_index)
    for which in (CR, SS, ST, CC):
        combine(1, which)

    tree_x.wait_sends()
    tree_t.wait_sends()
    wait_all(send_sems, GS, sg)
    for which in (ST, SS):
        wait_all(send_sems, MASS_OP + which - ST, masses.at[which - ST])
        wait_all(send_sems, own_op(which), own_logs.at[which - ST])
    for it in range(2):
        for which in range(4):
            wait_parts(send_sems, it, which)


def unpack_kernel(all_ref, cs_ref, ct_ref, ss_ref, st_ref):
    cs_ref[...] = all_ref[CR]
    ct_ref[...] = all_ref[CC]
    ss_ref[...] = all_ref[SS]
    st_ref[...] = all_ref[ST]


def body(size, source_desc, target_desc, source_mass, target_mass):
    count, group = source_desc.shape
    channels = target_desc.shape[1]
    flat = (size, LANES)
    ops = TREE_OP + 2 * (size // math.isqrt(size))
    wide = min(LSE_WIDE, count)
    whole = pl.BlockSpec(memory_space=pltpu.VMEM)
    packed = pl.pallas_call(
        functools.partial(body_kernel, size),
        out_shape=jax.ShapeDtypeStruct((4,) + flat, F32),
        in_specs=[pl.BlockSpec(memory_space=pl.ANY)] * 4,
        out_specs=whole,
        scratch_shapes=[
            pltpu.VMEM((group, count), BF16),
            pltpu.VMEM((channels, count), BF16),
            pltpu.VMEM(flat, BF16),
            pltpu.VMEM(flat, BF16),
            pltpu.VMEM((size, group, count), BF16),
            pltpu.VMEM((size, channels, LANES), BF16),
            pltpu.VMEM((size, channels, LANES), BF16),
            pltpu.VMEM((channels, count), F32),
            pltpu.VMEM((count, 256), BF16),
            pltpu.VMEM((count, 256), BF16),
            pltpu.VMEM((256, count), BF16),
            pltpu.VMEM((256, count), BF16),
            pltpu.VMEM((256, count), BF16),
            pltpu.VMEM((256, count), BF16),
            pltpu.VMEM((count, count), F32),
            pltpu.VMEM((count, count), F32),
            pltpu.VMEM((LSE_CHUNK, wide), F32),
            pltpu.VMEM((LSE_CHUNK, wide), F32),
            pltpu.VMEM(flat, F32),
            pltpu.VMEM(flat, F32),
            pltpu.VMEM(flat, F32),
            pltpu.VMEM((2, 4) + flat, F32),
            pltpu.VMEM((2, 4, size) + flat, F32),
            pltpu.VMEM((4,) + flat, F32),
            pltpu.VMEM((2, size, 1, LANES), F32),
            pltpu.VMEM((2, size, 1, LANES), F32),
            pltpu.SemaphoreType.DMA((4,)),
            pltpu.SemaphoreType.DMA((ops,)),
            pltpu.SemaphoreType.DMA((ops,)),
        ],
        compiler_params=pltpu.CompilerParams(
            collective_id=0, has_side_effects=True, vmem_limit_bytes=56 * 1024 * 1024
        ),
    )(
        source_desc.T,
        target_desc.T,
        source_mass.reshape(flat),
        target_mass.reshape(flat),
    )
    outs = pl.pallas_call(
        unpack_kernel,
        out_shape=[jax.ShapeDtypeStruct(flat, F32)] * 4,
        in_specs=[whole],
        out_specs=[whole] * 4,
    )(packed)
    return tuple(out.reshape(count) for out in outs)


def solution(mesh):
    return jax.shard_map(
        functools.partial(body, mesh.shape["row"]),
        mesh=mesh,
        in_specs=(P("row", "col"), P("col", None), P("row"), P("col")),
        out_specs=(P("row"), P("col"), P("row"), P("col")),
        check_vma=False,
    )
```

```python
import functools
import math

import jax
import jax.numpy as jnp
from jax import lax
from jax.experimental import pallas as pl
from jax.experimental.pallas import tpu as pltpu
from jax.sharding import PartitionSpec as P

MESH = pl.DeviceIdType.MESH
EPSILON = 0.25
REACH = 1.0
DAMPING = 1.0 / (1.0 + EPSILON / REACH)
LOG2E = math.log2(math.e)
LN2 = math.log(2.0)
SCALE = LOG2E / EPSILON
STEP = -0.5 * DAMPING
OUT = -0.5 * DAMPING * EPSILON * LN2
LANES = 128
F32 = jnp.float32
BF16 = jnp.bfloat16


def split3(value):
    high = value.astype(BF16).astype(F32)
    rest = value - high
    middle = rest.astype(BF16).astype(F32)
    low = (rest - middle).astype(BF16).astype(F32)
    return high, middle, low


def lane_block(k):
    return pl.ds(pl.multiple_of(k * LANES, LANES), LANES)


def side_rows(first, second, count):
    index = lax.broadcasted_iota(jnp.int32, (count, LANES), 0)
    rows = jnp.zeros((count, LANES), F32)
    for position, piece in enumerate(tuple(first) + tuple(second)):
        rows = jnp.where(index == position, piece, rows)
    return rows


def half_norm(points):
    return 0.5 * jnp.sum(points * points, axis=0, keepdims=True)


def right_block(b_ref, k, points):
    channels = points.shape[0]
    block = lane_block(k)
    narrow = points.astype(BF16)
    for copy in range(3):
        b_ref[copy * channels : (copy + 1) * channels, block] = narrow
    one = jnp.ones((1, LANES), F32)
    rows = side_rows((one, one, one), split3(-SCALE * half_norm(points)), 256 - 3 * channels)
    b_ref[3 * channels : 256, block] = rows.astype(BF16)


def left_block(a_ref, k, points, weight, whole):
    channels = points.shape[0]
    rows = pl.ds(pl.multiple_of(k * LANES, LANES), LANES)
    high, middle, low = split3(SCALE * points)
    if whole:
        a_ref[rows, 0:LANES] = jnp.concatenate([high, middle], axis=0).T.astype(BF16)
    one = jnp.ones((1, LANES), F32)
    side = side_rows(split3(weight - SCALE * half_norm(points)), (one, one, one), LANES - channels)
    a_ref[rows, LANES : 2 * LANES] = jnp.concatenate([low, side], axis=0).T.astype(BF16)


CHUNK = 256
LSE_WIDE = 1024
LSE_CHUNK = 128
KERNEL_WIDE = 1024
SUM_UNROLL = 4
SEND_UNROLL = 5
UNROLL = 8


def fold(value, op):
    return op(value.reshape(value.shape[0] // 8, 8, value.shape[1]), axis=0)


def emit(out_ref, j, row, wide):
    per = wide // LANES
    for t in range(per):
        piece = row[:, t * LANES : (t + 1) * LANES]
        out_ref[pl.ds(j * per + t, 1), :] = piece


def lse_pass(a_ref, b_ref, held, out_ref, part_index=None):
    count = b_ref.shape[1]
    wide = min(LSE_WIDE, count if part_index is None else count // 2)
    chunks = a_ref.shape[0] // LSE_CHUNK

    def column(j, carry):
        columns = pl.ds(pl.multiple_of(j * wide, wide), wide)
        right = b_ref[:, columns]

        def product(i):
            left = a_ref[i * LSE_CHUNK : (i + 1) * LSE_CHUNK, :]
            part = jnp.dot(left, right, preferred_element_type=F32)
            held[i % 2][:, 0:wide] = part
            return fold(part, jnp.max)

        top = jnp.full((8, wide), -1e30, F32)
        total = jnp.zeros((8, wide), F32)
        peak = product(0)
        for i in range(chunks):
            fresh = jnp.maximum(top, peak)
            if i + 1 < chunks:
                peak = product(i + 1)
            part = held[i % 2][:, 0:wide].reshape(LSE_CHUNK // 8, 8, wide)
            total = total * jnp.exp2(top - fresh) + jnp.sum(jnp.exp2(part - fresh[None]), axis=0)
            top = fresh
        peak = jnp.max(top, axis=0, keepdims=True)
        total = jnp.sum(total * jnp.exp2(top - peak), axis=0, keepdims=True)
        emit(out_ref, j, peak + jnp.log2(total), wide)
        return carry

    blocks = b_ref.shape[1] // wide
    if part_index is None:
        lax.fori_loop(0, blocks, column, 0)
    else:
        lax.fori_loop(part_index * blocks // 2, (part_index + 1) * blocks // 2, column, 0)


def kernel_pass(a_ref, b_ref, k_ref, out_ref):
    wide = min(KERNEL_WIDE, b_ref.shape[1])
    chunks = a_ref.shape[0] // CHUNK

    def step(j, carry):
        columns = pl.ds(pl.multiple_of(j * wide, wide), wide)
        right = b_ref[:, columns]
        total = jnp.zeros((8, wide), F32)
        for i in range(chunks):
            rows = slice(i * CHUNK, (i + 1) * CHUNK)
            part = jnp.exp2(jnp.dot(a_ref[rows, :], right, preferred_element_type=F32))
            k_ref[rows, columns] = part
            total = total + fold(part, jnp.sum)
        emit(out_ref, j, jnp.sum(total, axis=0, keepdims=True), wide)
        return carry

    lax.fori_loop(0, b_ref.shape[1] // wide, step, 0)


def weighted_pass(q_ref, k_ref, out_ref):
    def step(i, carry):
        rows = lane_block(i)
        total = jnp.zeros((LANES, LANES), F32)
        for t in range(k_ref.shape[1] // LANES):
            total = total + k_ref[rows, t * LANES : (t + 1) * LANES] * q_ref[t : t + 1, :]
        out_ref[pl.ds(i, 1), :] = jnp.sum(fold(total.T, jnp.sum), axis=0, keepdims=True)
        return carry

    lax.fori_loop(0, k_ref.shape[0] // LANES, step, 0, unroll=SUM_UNROLL)


CR, CC, ST, SS = 0, 1, 2, 3
GS = 0
FIRST_OP = 1
OWN_OP = FIRST_OP + 8
MASS_OP = OWN_OP + 2
HALF_OP = MASS_OP + 2
TREE_OP = HALF_OP + 1


def body_kernel(
    size,
    xs_hbm,
    yt_hbm,
    ms_hbm,
    mt_hbm,
    out_ref,
    xs_ref,
    yt_ref,
    ms_ref,
    mt_ref,
    xg,
    tg,
    sg,
    x32,
    ax,
    ay,
    bx,
    by,
    bs,
    bt,
    ks,
    kt,
    m0,
    m1,
    weights,
    lms,
    lmt,
    parts,
    inboxes,
    logs,
    own_logs,
    masses,
    local_sems,
    send_sems,
    recv_sems,
):
    row, col = lax.axis_index("row"), lax.axis_index("col")
    place = {"row": row, "col": col}

    def peer(axis, k):
        return lax.rem(place[axis] + k, size)

    barrier = pltpu.get_barrier_semaphore()

    def greet(k, carry):
        for axis in ("col", "row"):
            pl.semaphore_signal(
                barrier, inc=1, device_id={axis: peer(axis, k)}, device_id_type=MESH
            )
        return carry

    lax.fori_loop(1, size, greet, 0)

    loads = [
        pltpu.make_async_copy(source, target, local_sems.at[index])
        for index, (source, target) in enumerate(
            ((yt_hbm, yt_ref), (mt_hbm, mt_ref), (ms_hbm, ms_ref), (xs_hbm, xs_ref))
        )
    ]
    for load in loads:
        load.start()

    def send_all(op, axis, source, slot):
        def one(i, carry):
            half = (i + 1) // 2
            other = peer(axis, size // 2 + half * (2 * lax.rem(i, 2) - 1))
            pltpu.make_async_remote_copy(
                src_ref=source,
                dst_ref=slot,
                send_sem=send_sems.at[op],
                recv_sem=recv_sems.at[op],
                device_id={axis: other},
                device_id_type=MESH,
            ).start()
            return carry

        lax.fori_loop(0, size - 1, one, 0, unroll=SEND_UNROLL)

    inner = math.isqrt(size)
    outer = size // inner
    at_outer, at_inner = col // inner, lax.rem(col, inner)

    def spot(out_index, in_index):
        return in_index * outer + out_index

    def tree_send(op, box, slot, device):
        pltpu.make_async_remote_copy(
            src_ref=box.at[slot],
            dst_ref=box.at[slot],
            send_sem=send_sems.at[op],
            recv_sem=recv_sems.at[op],
            device_id={"col": device},
            device_id_type=MESH,
        ).start()

    class Tree:
        def __init__(self, first_op, box):
            self.first_op, self.box = first_op, box

        def start(self):
            slot = spot(at_outer, at_inner)
            for k in sorted(range(1, outer), key=lambda k: -min(k, outer - k)):
                other = lax.rem(at_outer + k, outer)
                tree_send(self.first_op + k, self.box, slot, other * inner + at_inner)
            self.spread(slot)

        def spread(self, slot):
            for k in range(1, inner):
                other = lax.rem(at_inner + k, inner)
                tree_send(self.first_op, self.box, slot, at_outer * inner + other)

        def forward(self, k):
            slot = spot(lax.rem(at_outer + outer - k, outer), at_inner)
            wait_one(recv_sems, self.first_op + k, self.box.at[slot])
            self.spread(slot)

        def wait(self, sems):
            wait_one(sems, self.first_op, self.box.at[pl.ds(0, outer * (inner - 1))])

        def wait_sends(self):
            self.wait(send_sems)
            for k in range(1, outer):
                wait_one(send_sems, self.first_op + k, self.box.at[0])

    def wait_one(sems, op, target):
        pltpu.make_async_copy(target, target, sems.at[op]).wait()

    def wait_all(sems, op, target):
        wait_one(sems, op, target.at[pl.ds(0, size - 1)])

    def blocks(step):
        def run(k, carry):
            step(k)
            return carry

        lax.fori_loop(0, size, run, 0, unroll=UNROLL)

    for load in loads:
        load.wait()
    log_mass_x = jnp.log2(ms_ref[...].astype(F32))
    log_mass_y = jnp.log2(mt_ref[...].astype(F32))
    lms[...] = log_mass_x
    lmt[...] = log_mass_y

    def prepare_y(k):
        points = yt_ref[:, lane_block(k)].astype(F32)
        right_block(by, k, points)
        left_block(ay, k, points, lmt[pl.ds(k, 1), :], True)

    blocks(prepare_y)
    mine = spot(at_outer, at_inner)
    tg[mine] = yt_ref[:, lane_block(row)]
    xg[mine] = xs_ref[...]
    slot_of = {ST: mine, SS: row}
    piece_of = {ST: row, SS: col}
    for which, source in ((ST, lmt), (SS, lms)):
        masses[which - ST, slot_of[which]] = source[pl.ds(piece_of[which], 1), :]

    pl.semaphore_wait(barrier, 2 * (size - 1))
    tree_x, tree_t = Tree(TREE_OP, xg), Tree(TREE_OP + outer, tg)
    by_distance = sorted(range(1, outer), key=lambda k: min(k, outer - k))
    tree_x.start()
    for k in by_distance:
        tree_x.forward(k)
    tree_t.start()
    for which, axis in ((ST, "col"), (SS, "row")):
        slot = masses.at[which - ST, slot_of[which]]
        send_all(MASS_OP + which - ST, axis, slot, slot)

    tree_x.wait(recv_sems)
    group = xs_ref.shape[0]
    for c in range(size):
        block = xg[spot(c // inner, c % inner)]
        x32[c * group : (c + 1) * group, :] = block.astype(F32)

    def prepare_x(k):
        points = x32[:, lane_block(k)]
        right_block(bx, k, points)
        left_block(ax, k, points, lms[pl.ds(k, 1), :], True)

    blocks(prepare_x)
    channels = x32.shape[0]
    send_all(GS, "row", bx.at[0:channels, lane_block(col)], sg.at[row])
    sg[row] = bx[0:channels, lane_block(col)]

    AXIS = (("col", "row", "col", "row"), ("col", "row", "row", "col"))

    def op_of(it, which):
        return FIRST_OP + 4 * it + which

    def send_parts(it, which):
        axis = AXIS[it][which]
        part, inbox = parts.at[it, which], inboxes.at[it, which]
        me = place[axis]
        send_all(op_of(it, which), axis, part, inbox.at[me])
        inbox[me] = part[...]

    def own_op(which):
        return OWN_OP + which - ST

    def send_own(which):
        box, axis = own_logs.at[which - ST], AXIS[1][which]
        me = place[axis]
        box[me] = logs[which, pl.ds(slot_of[which], 1), :]
        send_all(own_op(which), axis, box.at[me], box.at[me])

    half = size // 2

    def send_half(part_index):
        rows = pl.ds(part_index * half, half)
        part, slot = parts.at[1, CC, rows], inboxes.at[1, CC, row, rows]
        send_all(op_of(1, CC) if part_index == 0 else HALF_OP, "row", part, slot)
        if part_index == 1:
            inboxes[1, CC, row] = parts[1, CC]

    def wait_parts(sems, it, which):
        inbox = inboxes.at[it, which]
        if (it, which) == (1, CC):
            some = inbox.at[pl.ds(0, size - 1), pl.ds(0, half)]
            wait_one(sems, op_of(it, which), some)
            wait_one(sems, HALF_OP, some)
        else:
            wait_all(sems, op_of(it, which), inbox)

    def combine(it, which):
        inbox = inboxes.at[it, which]
        wait_parts(recv_sems, it, which)
        values = inbox[...]
        if which in (CR, CC):
            top = jnp.max(values, axis=0)
            total = top + jnp.log2(jnp.sum(jnp.exp2(values - top[None]), axis=0))
        else:
            total = jnp.log2(jnp.sum(values, axis=0))
            if it == 1:
                total = total - (lms if which == SS else lmt)[...]
        if it == 0:
            logs[which] = total
            if which in (ST, SS):
                send_own(which)
        elif which in (CR, CC):
            out_ref[which] = (0.5 * OUT) * logs[which] + OUT * total
        else:
            box = own_logs.at[which - ST]
            wait_all(recv_sems, own_op(which), box)
            for k in range(size):
                out_ref[which, k : k + 1, :] = (0.5 * OUT) * box[k] + OUT * total[k : k + 1, :]

    def prepare_right(b_ref, inbox):
        blocks(lambda k: right_block(b_ref, k, inbox[k].astype(F32)))

    def reweight(a_ref, b_ref, mass, which):
        def step(k):
            points = b_ref[0:channels, lane_block(k)].astype(F32)
            one = pl.ds(k, 1)
            left_block(a_ref, k, points, mass[one, :] + STEP * logs[which, one, :], False)

        blocks(step)

    def row_sums(k_ref, which):
        box = masses.at[which - ST]
        wait_all(recv_sems, MASS_OP + which - ST, box)
        for k in range(size):
            weights[k : k + 1, :] = jnp.exp2(box[k] + STEP * logs[which, k : k + 1, :])
        weighted_pass(weights, k_ref, parts.at[1, which])

    held = (m0, m1)
    lse_pass(ax, by, held, parts.at[0, CC])
    send_parts(0, CC)
    for k in by_distance:
        tree_t.forward(k)
    lse_pass(ay, bx, held, parts.at[0, CR])
    send_parts(0, CR)
    tree_t.wait(recv_sems)
    prepare_right(bt, tg)
    kernel_pass(ay, bt, kt, parts.at[0, ST])
    send_parts(0, ST)
    wait_all(recv_sems, GS, sg)
    prepare_right(bs, sg)
    kernel_pass(ax, bs, ks, parts.at[0, SS])
    send_parts(0, SS)
    combine(0, CC)
    reweight(ay, by, lmt, CC)
    lse_pass(ay, bx, held, parts.at[1, CR])
    send_parts(1, CR)
    combine(0, ST)
    row_sums(kt, ST)
    send_parts(1, ST)
    combine(0, SS)
    row_sums(ks, SS)
    send_parts(1, SS)
    combine(0, CR)
    reweight(ax, bx, lms, CR)
    for part_index in range(2):
        lse_pass(ax, by, held, parts.at[1, CC], part_index)
        send_half(part_index)
    for which in (CR, SS, ST, CC):
        combine(1, which)

    tree_x.wait_sends()
    tree_t.wait_sends()
    wait_all(send_sems, GS, sg)
    for which in (ST, SS):
        wait_all(send_sems, MASS_OP + which - ST, masses.at[which - ST])
        wait_all(send_sems, own_op(which), own_logs.at[which - ST])
    for it in range(2):
        for which in range(4):
            wait_parts(send_sems, it, which)


def unpack_kernel(all_ref, cs_ref, ct_ref, ss_ref, st_ref, sems):
    copies = [
        pltpu.make_async_copy(all_ref.at[which], target, sems.at[which])
        for which, target in ((CR, cs_ref), (CC, ct_ref), (SS, ss_ref), (ST, st_ref))
    ]
    for copy in copies:
        copy.start()
    for copy in copies:
        copy.wait()


def body(size, source_desc, target_desc, source_mass, target_mass):
    count, group = source_desc.shape
    channels = target_desc.shape[1]
    flat = (size, LANES)
    ops = TREE_OP + 2 * (size // math.isqrt(size))
    wide = min(LSE_WIDE, count)
    whole = pl.BlockSpec(memory_space=pltpu.VMEM)
    packed = pl.pallas_call(
        functools.partial(body_kernel, size),
        out_shape=jax.ShapeDtypeStruct((4,) + flat, F32),
        in_specs=[pl.BlockSpec(memory_space=pl.ANY)] * 4,
        out_specs=whole,
        scratch_shapes=[
            pltpu.VMEM((group, count), BF16),
            pltpu.VMEM((channels, count), BF16),
            pltpu.VMEM(flat, BF16),
            pltpu.VMEM(flat, BF16),
            pltpu.VMEM((size, group, count), BF16),
            pltpu.VMEM((size, channels, LANES), BF16),
            pltpu.VMEM((size, channels, LANES), BF16),
            pltpu.VMEM((channels, count), F32),
            pltpu.VMEM((count, 256), BF16),
            pltpu.VMEM((count, 256), BF16),
            pltpu.VMEM((256, count), BF16),
            pltpu.VMEM((256, count), BF16),
            pltpu.VMEM((256, count), BF16),
            pltpu.VMEM((256, count), BF16),
            pltpu.VMEM((count, count), F32),
            pltpu.VMEM((count, count), F32),
            pltpu.VMEM((LSE_CHUNK, wide), F32),
            pltpu.VMEM((LSE_CHUNK, wide), F32),
            pltpu.VMEM(flat, F32),
            pltpu.VMEM(flat, F32),
            pltpu.VMEM(flat, F32),
            pltpu.VMEM((2, 4) + flat, F32),
            pltpu.VMEM((2, 4, size) + flat, F32),
            pltpu.VMEM((4,) + flat, F32),
            pltpu.VMEM((2, size, 1, LANES), F32),
            pltpu.VMEM((2, size, 1, LANES), F32),
            pltpu.SemaphoreType.DMA((4,)),
            pltpu.SemaphoreType.DMA((ops,)),
            pltpu.SemaphoreType.DMA((ops,)),
        ],
        compiler_params=pltpu.CompilerParams(
            collective_id=0, has_side_effects=True, vmem_limit_bytes=56 * 1024 * 1024
        ),
    )(
        source_desc.T,
        target_desc.T,
        source_mass.reshape(flat),
        target_mass.reshape(flat),
    )
    outs = pl.pallas_call(
        unpack_kernel,
        out_shape=[jax.ShapeDtypeStruct(flat, F32)] * 4,
        in_specs=[pl.BlockSpec(memory_space=pl.ANY)],
        out_specs=[pl.BlockSpec(memory_space=pl.ANY)] * 4,
        scratch_shapes=[pltpu.SemaphoreType.DMA((4,))],
        compiler_params=pltpu.CompilerParams(vmem_limit_bytes=56 * 1024 * 1024),
    )(packed)
    return tuple(out.reshape(count) for out in outs)


def solution(mesh):
    return jax.shard_map(
        functools.partial(body, mesh.shape["row"]),
        mesh=mesh,
        in_specs=(P("row", "col"), P("col", None), P("row"), P("col")),
        out_specs=(P("row"), P("col"), P("row"), P("col")),
        check_vma=False,
    )
```
